128 devices in a mesh: grp: 8 (over x_lo, z), tp: 16 (over y, x_hi, core).
Axes of the slice: x: 4 (x_hi: 2, x_lo: 2; x = x_hi * 2 + x_lo), y: 4, z: 4, core: 2. Of those that a mesh axis runs over, the one named last changes fastest.
Arguments:
- activations: bfloat16 [12288, 5120], P('grp', 'tp'), may hold values from -6 to 6
- norm_gain: float32 [5120], replicated, may hold values from 0.1 to 1.9
- query_gain: float32 [128], replicated, may hold values from 0.1 to 1.9
- key_gain: float32 [128], replicated, may hold values from 0.1 to 1.9
- query_weight: bfloat16 [5120, 8192], P('grp', 'tp'), may hold values from -0.078125 to 0.078125
- keyval_weight: bfloat16 [5120, 2048], P('grp', 'tp'), may hold values from -0.078125 to 0.078125
- lengths: int32 [8, 8], replicated, may hold values from 1 to 1529, as said below
Outputs:
- key_value_cache: bfloat16 [12288, 2048], P('grp', 'tp')
- attention_context: bfloat16 [12288, 8192], P('grp', 'tp')
The draws below stay inside these ranges and needn't reach their ends.
Inputs may be any that keep to these rules, and one draw needn't show every extreme that they name: `lengths`: every length is positive. A group's block of 128 rows (rows k * 128 to (k + 1) * 128 - 1 of the group) is live if it holds a row of one of the group's rollouts. The live blocks of all groups number exactly 48. In one group all 1536 rows are used: one of its rollouts has 1529 rows and the others one row each.
All inputs are finite; a program needn't handle non-finite values.
Results may differ from the reference program's by a relative error of at most 0.0077.
Values may be sent and summed in bfloat16 or wider, within the bound.
A program may use at most 128 MiB of HBM per device.

```python
import math
import jax
import jax.numpy as jnp
from jax import lax

D = 5120
QH = 64
KVH = 8
HD = 128
TOK_GRP = 1536
ROLLOUTS = 8
BLK = 128
GROUPS = 8
TOKENS = 12288


def draw_lengths(key, part):
    key = jax.random.fold_in(key, 7)
    first_key, second_key, third_key, fourth_key, fifth_key = jax.random.split(key, 5)
    blocks_each = TOK_GRP // BLK
    others = GROUPS - 1
    extra = GROUPS * blocks_each // 2 - blocks_each - others
    pool_size = others * (blocks_each - 1)
    order = jax.random.permutation(first_key, pool_size)
    picked = (order < extra).astype(jnp.int32)
    owner_of = jnp.arange(pool_size) // (blocks_each - 1)
    counts = jnp.sum(jnp.where(owner_of[None, :] == jnp.arange(others)[:, None], picked[None, :], 0), axis=1)
    full_group = jax.random.randint(second_key, (), 0, GROUPS)
    group_ids = jnp.arange(GROUPS)
    shifted = jnp.clip(group_ids - (group_ids > full_group).astype(jnp.int32), 0, others - 1)
    live_count = jnp.where(group_ids == full_group, blocks_each, 1 + counts[shifted])
    spare = jax.random.randint(third_key, (GROUPS,), 0, BLK - ROLLOUTS + 1)
    used_rows = (live_count * BLK - spare).astype(jnp.int32)
    group_keys = jax.random.split(fourth_key, GROUPS)

    def split_group(one_key, total_rows):
        scores = jax.random.permutation(one_key, TOK_GRP).astype(jnp.int32)
        places = jnp.arange(TOK_GRP, dtype=jnp.int32)
        usable = (places >= 1) & (places < total_rows)
        ranked = jnp.where(usable, scores, -1 - places)
        cut_points = jnp.sort(lax.top_k(ranked, ROLLOUTS - 1)[1].astype(jnp.int32))
        bounds = jnp.concatenate([jnp.zeros((1,), jnp.int32), cut_points, total_rows[None]])
        return bounds[1:] - bounds[:-1]
    split = jax.vmap(split_group)(group_keys, used_rows).astype(jnp.int32)
    long_index = jax.random.randint(fifth_key, (), 0, ROLLOUTS)
    full_row = jnp.where(jnp.arange(ROLLOUTS) == long_index, TOK_GRP - ROLLOUTS + 1, 1).astype(jnp.int32)
    return jnp.where((group_ids == full_group)[:, None], full_row[None, :], split).astype(jnp.int32)


def steps_of(stream_key, shape, pieces, smallest, top_value):
    gain = 1.0
    for dim, blocks in pieces:
        steps = jax.random.uniform(jax.random.fold_in(jax.random.fold_in(stream_key, 6), dim), (blocks,), jnp.float32, smallest / len(pieces), top_value / len(pieces))
        gain = gain * jnp.repeat(jnp.exp(steps), shape[dim] // blocks).reshape((-1,) + (1,) * (len(shape) - 1 - dim))
    return gain


def normal_values(own_key, shape, scale, limit, pieces=(), held_as=jnp.bfloat16):
    loudness = steps_of(own_key, shape, pieces, -0.22, 0.18) if pieces else 1.0
    result = jax.random.normal(own_key, shape, jnp.float32) * scale * loudness
    return jnp.minimum(jnp.maximum(result, -limit), limit).astype(held_as)


def setup_inputs(seed: int = 0) -> dict:
    key_of = jax.random.split(jax.random.key(seed), 8)
    activations = normal_values(key_of[0], (TOKENS, D), 1.0, 6.0, ((0, 8), (1, 16)))
    norm_gain = jnp.clip(1.0 + 0.18 * jax.random.normal(key_of[1], (D,), jnp.float32), 0.1, 1.9)
    query_gain = jnp.clip(1.0 + 0.18 * jax.random.normal(key_of[2], (HD,), jnp.float32), 0.1, 1.9)
    key_gain = jnp.clip(1.0 + 0.18 * jax.random.normal(key_of[3], (HD,), jnp.float32), 0.1, 1.9)
    query_weight = normal_values(key_of[4], (D, QH * HD), D ** -0.5, 0.078125, ((0, 8), (1, 16)))
    keyval_weight = normal_values(key_of[5], (D, 2 * KVH * HD), D ** -0.5, 0.078125, ((0, 8), (1, 16)))
    lengths = draw_lengths(jax.random.fold_in(key_of[7], 71), 0)
    return dict(activations=activations, norm_gain=norm_gain, query_gain=query_gain, key_gain=key_gain, query_weight=query_weight, keyval_weight=keyval_weight, lengths=lengths)


eps = 1e-06
theta_log = math.log(1000000.0)

def row_layout(lengths_row, row_ids):
    rollout_ends = jnp.cumsum(lengths_row)
    passed = row_ids[:, None] >= rollout_ends[None, :]
    segment = lax.optimization_barrier(jnp.sum(passed.astype(jnp.int32), axis=1))
    before = lax.optimization_barrier(jnp.sum(jnp.where(passed, lengths_row[None, :], 0), axis=1))
    position = (row_ids - before).astype(jnp.int32)
    is_live = segment < lengths_row.shape[0]
    return (segment, position, is_live)

def head_norm(values, gains):
    return values * lax.rsqrt(lax.optimization_barrier(jnp.mean(values * values, axis=-1, keepdims=True)) + eps) * gains

def rotate(values, position):
    half_dim = values.shape[-1] // 2
    inverse = jnp.exp(jnp.arange(half_dim, dtype=jnp.float32) * (-2.0 * theta_log / values.shape[-1]))
    angles = position.astype(jnp.float32)[:, None] * inverse[None, :]
    cosines = jnp.cos(angles)[:, None, :]
    sines = jnp.sin(angles)[:, None, :]
    lower_half = values[..., :half_dim]
    upper_half = values[..., half_dim:]
    return jnp.concatenate([lower_half * cosines - upper_half * sines, upper_half * cosines + lower_half * sines], axis=-1)

def attend_head(query, key_rows, value_rows, segment, position, is_live):
    scores = jnp.einsum('qgd,kd->qgk', query.astype(jnp.float32), key_rows.astype(jnp.float32)) * (1.0 / math.sqrt(HD))
    allowed = (segment[:, None] == segment[None, :]) & (position[None, :] <= position[:, None])
    allowed = (allowed & is_live[:, None] & is_live[None, :])[:, None, :]
    scores = jnp.where(allowed, scores, -1e+30)
    row_peak = lax.optimization_barrier(jnp.max(scores, axis=2, keepdims=True))
    weight = jnp.where(allowed, jnp.exp(scores - row_peak), 0.0)
    denominator = jnp.where(is_live[:, None, None], lax.optimization_barrier(jnp.sum(weight, axis=2, keepdims=True)), 1.0)
    probability = (weight / denominator).astype(jnp.bfloat16)
    return jnp.einsum('qgk,kd->qgd', probability.astype(jnp.float32), value_rows.astype(jnp.float32)).astype(jnp.bfloat16)

def reference(activations, norm_gain, query_gain, key_gain, query_weight, keyval_weight, lengths):
    caches = []
    contexts = []
    for group_id in range(GROUPS):
        rows_in = activations[group_id * TOK_GRP:(group_id + 1) * TOK_GRP]
        segment, position, is_live = row_layout(lengths[group_id], jnp.arange(TOK_GRP, dtype=jnp.int32))
        as_float = rows_in.astype(jnp.float32)
        inv_rms = lax.rsqrt(lax.optimization_barrier(jnp.mean(as_float * as_float, axis=1, keepdims=True)) + eps)
        normed = (as_float * inv_rms * norm_gain[None, :]).astype(jnp.bfloat16)
        query_sum = jnp.dot(normed, query_weight, preferred_element_type=jnp.float32)
        keyval_sum = jnp.dot(normed, keyval_weight, preferred_element_type=jnp.float32).reshape(TOK_GRP, KVH, 2, HD)
        query = rotate(head_norm(query_sum.reshape(TOK_GRP, QH, HD), query_gain), position).astype(jnp.bfloat16)
        key_rows = rotate(head_norm(keyval_sum[:, :, 0], key_gain), position).astype(jnp.bfloat16)
        value_rows = keyval_sum[:, :, 1].astype(jnp.bfloat16)
        key_rows = jnp.where(is_live[:, None, None], key_rows, 0)
        value_rows = jnp.where(is_live[:, None, None], value_rows, 0)
        caches.append(jnp.stack([key_rows, value_rows], axis=2).reshape(TOK_GRP, 2 * KVH * HD))
        grouped = jnp.moveaxis(query.reshape(TOK_GRP, KVH, QH // KVH, HD), 1, 0)

        def per_head(operands):
            return attend_head(operands[0], operands[1], operands[2], segment, position, is_live)
        heads_out = lax.map(per_head, (grouped, jnp.moveaxis(key_rows, 1, 0), jnp.moveaxis(value_rows, 1, 0)))
        contexts.append(jnp.moveaxis(heads_out, 0, 1).reshape(TOK_GRP, QH * HD))
    return (jnp.concatenate(caches, axis=0), jnp.concatenate(contexts, axis=0))
```

```python
import functools
import math

import jax
import jax.numpy as jnp
import numpy as np
from jax import lax
from jax.experimental import pallas as pl
from jax.experimental.pallas import tpu as pltpu
from jax.sharding import PartitionSpec as P

EPS = 1e-06
THETA = 1000000.0
MESH = pl.DeviceIdType.MESH
HD = 128
ROWS = 1536
CH = 128
HALF = CH // 2
NCH = ROWS // CH
FEAT = 640
WROWS = 640
KH = 320
NW = 10
KTILE = 256
T_KV, T_Q01, T_Q23 = 6, 9, 13


def kernel(
    len_ref, x_ref, gain_ref, freq_ref, qg_ref, kg_ref, wq_ref, wkv_ref,
    cache_ref, ctx_ref,
    xbuf, wbuf, pbuf, ss, ssacc, tinv, cosb, sinb, kbuf, vbuf, acc,
    swap_s, swap_r, ss_s, ss_r, loc_s,
    ax_s, ax_r, ay_s, ay_r, ar_s, ar_r, ad_s, ad_r,
    wx_s, wx_r, wz_s, wz_r, wr_s, wr_r, wd_s, wd_r,
):
    g = lax.axis_index("grp")
    t = lax.axis_index("tp")
    core = lax.rem(t, 2)
    chip = t // 2
    xchip = chip + 1 - 2 * lax.rem(chip, 2)

    def chip_of(base, step):
        return lax.rem(base + 2 * step, 8)

    def tp_dev(c, k):
        return (g, c * 2 + k)

    up, down = tp_dev(chip_of(chip, 1), core), tp_dev(chip_of(chip, 3), core)
    across, twin = tp_dev(xchip, core), tp_dev(chip, 1 - core)
    gx = lax.rem(g + 4, 8)

    def ring(base, step):
        return (base // 4) * 4 + lax.rem(lax.rem(base, 4) + step, 4)

    zup, zdown, wacross = (ring(g, 1), t), (ring(g, 3), t), (gx, t)

    bar = pltpu.get_barrier_semaphore()

    def greet(k, c):
        pl.semaphore_signal(bar, inc=1, device_id=(g, lax.rem(t + k, 16)), device_id_type=MESH)
        return c

    lax.fori_loop(1, 16, greet, 0)
    for d in (zup, zdown, wacross):
        pl.semaphore_signal(bar, inc=1, device_id=d, device_id_type=MESH)

    own_w = pl.multiple_of(g * WROWS, WROWS)
    c1 = pltpu.make_async_copy(wq_ref, wbuf.at[pl.ds(own_w, WROWS), pl.ds(2 * HD, 4 * HD)], loc_s.at[0])
    c2 = pltpu.make_async_copy(
        wkv_ref, wbuf.at[pl.ds(own_w, WROWS), pl.ds(pl.multiple_of(core * HD, HD), HD)], loc_s.at[1]
    )
    c1.start()
    c2.start()
    kbuf[...] = jnp.zeros_like(kbuf)
    vbuf[:, :HD] = jnp.zeros((ROWS, HD), jnp.bfloat16)
    vbuf[:, HD:] = jnp.ones((ROWS, HD), jnp.bfloat16)
    pl.semaphore_wait(bar, 18)

    def rcopy(src, dst, s, r, dev):
        return pltpu.make_async_remote_copy(
            src_ref=src, dst_ref=dst, send_sem=s, recv_sem=r, device_id=dev, device_id_type=MESH
        )

    swap = rcopy(x_ref.at[:, 1 - core], pbuf, swap_s, swap_r, twin)
    swap.start()

    def wview(owner, i, part=None):
        j = i // 2
        col = pl.multiple_of(jnp.where(j == 0, core * HD, HD + HD * j), HD)
        row = owner * WROWS + lax.rem(i, 2) * KH
        n = KH
        if part is not None:
            n = KH // 2
            row = row + part * n
        return wbuf.at[pl.ds(pl.multiple_of(row, 32), n), pl.ds(col, HD)]

    def wmsg(owner, i, s, r, dev, part=None):
        v = wview(owner, i, part)
        return rcopy(v, v, s, r, dev)

    def w_x(i, owner):
        return wmsg(owner, i, wx_s.at[i], wx_r.at[i], wacross)

    def w_z(i, cls, d, owner):
        k = cls * 2 + d
        return wmsg(owner, i, wz_s.at[i, k], wz_r.at[i, k], (zup, zdown)[d])

    def w_r(i, cls, d, owner):
        k = cls * 2 + d
        return wmsg(owner, i, wr_s.at[i, k], wr_r.at[i, k], (zup, zdown)[d], part=d)

    def kvview(i, slot, col):
        row = slot * WROWS + i * KH
        return wbuf.at[pl.ds(pl.multiple_of(row, 32), KH), pl.ds(pl.multiple_of(col * HD, HD), HD)]

    def w_d(i, owner, col):
        v = kvview(i, owner, col)
        return rcopy(v, v, wd_s.at[i, owner], wd_r.at[i, owner], twin)

    def w_share(i, owner):
        @pl.when(i < 2)
        def _():
            w_d(i, owner, core).start()

    def w0(i):
        w_x(i, g).start()
        w_z(i, 0, 0, g).start()
        w_z(i, 0, 1, g).start()
        w_share(i, g)

    def w1(i):
        w_x(i, gx).wait_recv()
        w_z(i, 1, 0, gx).start()
        w_z(i, 1, 1, gx).start()
        w_share(i, gx)
        lo, hi = ring(g, 3), ring(g, 1)
        w_z(i, 0, 0, lo).wait_recv()
        w_r(i, 0, 0, lo).start()
        w_share(i, lo)
        w_z(i, 0, 1, hi).wait_recv()
        w_r(i, 0, 1, hi).start()
        w_share(i, hi)

    def w2(i):
        lo, hi = ring(gx, 3), ring(gx, 1)
        w_z(i, 1, 0, lo).wait_recv()
        w_r(i, 1, 0, lo).start()
        w_share(i, lo)
        w_z(i, 1, 1, hi).wait_recv()
        w_r(i, 1, 1, hi).start()
        w_share(i, hi)

    def w3(i):
        for cls, base in ((0, g), (1, gx)):
            far = ring(base, 2)
            w_r(i, cls, 0, far).wait_recv()
            w_r(i, cls, 1, far).wait_recv()
            w_share(i, far)

    def w4(i):
        @pl.when(i < 2)
        def _():
            def one(owner, c):
                w_d(i, owner, 1 - core).wait_recv()
                return c

            lax.fori_loop(0, 8, one, 0)

    def aview(owner, i, k, part=None):
        row = i * CH + k * HALF
        n = HALF
        if part is not None:
            n = HALF // 2
            row = row + part * n
        return xbuf.at[
            pl.ds(pl.multiple_of(row, 32), n), pl.ds(pl.multiple_of(owner * FEAT, FEAT), FEAT)
        ]

    def amsg(owner, i, s, r, dev, part=None, k=None):
        v = aview(owner, i, core if k is None else k, part)
        return rcopy(v, v, s, r, dev)

    def a_x(i, owner):
        return amsg(owner, i, ax_s.at[i], ax_r.at[i], across)

    def a_y(i, cls, d, owner):
        k = cls * 2 + d
        return amsg(owner, i, ay_s.at[i, k], ay_r.at[i, k], (up, down)[d])

    def a_r(i, cls, d, owner):
        k = cls * 2 + d
        return amsg(owner, i, ar_s.at[i, k], ar_r.at[i, k], (up, down)[d], part=d)

    def a_d(i, owner, k):
        return amsg(owner, i, ad_s.at[i, owner], ad_r.at[i, owner], twin, k=k)

    def a0(i):
        a_y(i, 0, 0, chip).start()
        a_y(i, 0, 1, chip).start()
        a_x(i, chip).start()
        a_d(i, chip, core).start()

    def a1(i):
        a_x(i, xchip).wait_recv()
        a_y(i, 1, 0, xchip).start()
        a_y(i, 1, 1, xchip).start()
        a_d(i, xchip, core).start()
        lo, hi = chip_of(chip, 3), chip_of(chip, 1)
        a_y(i, 0, 0, lo).wait_recv()
        a_r(i, 0, 0, lo).start()
        a_d(i, lo, core).start()
        a_y(i, 0, 1, hi).wait_recv()
        a_r(i, 0, 1, hi).start()
        a_d(i, hi, core).start()

    def a2(i):
        lo, hi = chip_of(xchip, 3), chip_of(xchip, 1)
        a_y(i, 1, 0, lo).wait_recv()
        a_r(i, 1, 0, lo).start()
        a_d(i, lo, core).start()
        a_y(i, 1, 1, hi).wait_recv()
        a_r(i, 1, 1, hi).start()
        a_d(i, hi, core).start()

    def a3(i):
        for cls, base in ((0, chip), (1, xchip)):
            far = chip_of(base, 2)
            a_r(i, cls, 0, far).wait_recv()
            a_r(i, cls, 1, far).wait_recv()
            a_d(i, far, core).start()

    def a4(i):
        def one(owner, c):
            a_d(i, owner, 1 - core).wait_recv()
            return c

        lax.fori_loop(0, 8, one, 0)

    own_f = pl.multiple_of(chip * FEAT, FEAT)

    def merge(i):
        mine = x_ref[i, core].astype(jnp.float32)
        other = pbuf[i].astype(jnp.float32)
        first = jnp.where(core == 0, mine, other)
        second = jnp.where(core == 0, other, mine)
        both = jnp.concatenate([first, second], axis=1)
        squares = jnp.sum(both * both, axis=1, keepdims=True)
        scaled = (both * gain_ref[:, pl.ds(own_f, FEAT)]).astype(jnp.bfloat16)
        row = pl.multiple_of(i * CH + core * HALF, 32)
        xbuf[pl.ds(row, HALF), pl.ds(own_f, FEAT)] = scaled
        lane = lax.broadcasted_iota(jnp.int32, (HALF, CH), 1)
        at = pl.ds(pl.multiple_of(core * HALF, HALF), HALF)
        ssacc[at, :] = jnp.where(lane == i, squares, ssacc[at, :])

    ssacc[...] = jnp.zeros_like(ssacc)
    c2.wait()
    c1.wait()
    w0(0)
    w0(1)
    swap.wait_recv()
    merge(0)
    a0(0)
    merge(1)
    a0(1)

    def merge_rest(i, c):
        merge(i)
        return c

    lax.fori_loop(2, NCH, merge_rest, 0)
    ss[t] = jnp.transpose(ssacc[...])[:16]

    def ss_msg(slot, k):
        return rcopy(ss.at[slot], ss.at[slot], ss_s.at[k], ss_r.at[slot], (g, lax.rem(t + k, 16)))

    def ss_go(k, c):
        ss_msg(t, k).start()
        return c

    lax.fori_loop(1, 16, ss_go, 0)

    ends = []
    total = 0
    for r in range(8):
        total = total + len_ref[g, r]
        ends.append(total)

    def starts_of(rows):
        start = jnp.zeros_like(rows)
        for r in range(8):
            start = start + jnp.where(rows >= ends[r], len_ref[g, r], 0)
        return start

    def rows_of(u, n, lanes):
        return u * CH + lax.broadcasted_iota(jnp.int32, (n, lanes), 0)

    def trig(u, c):
        rows = rows_of(u, CH, HD)
        angle = (rows - starts_of(rows)).astype(jnp.float32) * freq_ref[...]
        lane = lax.broadcasted_iota(jnp.int32, (CH, HD), 1)
        at = pl.ds(pl.multiple_of(u * CH, CH), CH)
        cosb[at, :] = jnp.cos(angle)
        sinb[at, :] = jnp.where(lane < HD // 2, -1.0, 1.0) * jnp.sin(angle)
        return c

    lax.fori_loop(0, NCH, trig, 0)

    def at_rows(u):
        return pl.ds(pl.multiple_of(u * CH, CH), CH)

    def inv_of(u):
        lane = lax.broadcasted_iota(jnp.int32, (CH, CH), 1)
        return jnp.sum(jnp.where(lane == u, tinv[...], 0.0), axis=1, keepdims=True)

    def finish(a, inv, gains, u):
        m = jnp.mean(a * a, axis=1, keepdims=True)
        a = a * (inv * lax.rsqrt(inv * inv * m + EPS)) * gains
        return a * cosb[at_rows(u), :] + pltpu.roll(a, HD // 2, 1) * sinb[at_rows(u), :]

    def project(u, col):
        return jnp.dot(
            xbuf[at_rows(u), :], wbuf[:, pl.ds(col, 2 * HD)], preferred_element_type=jnp.float32
        )

    def do_kv(u, c):
        r = project(u, 0)
        inv = inv_of(u)
        live = rows_of(u, CH, HD) < total
        key = jnp.where(live, finish(r[:, :HD], inv, kg_ref[...], u), 0.0).astype(jnp.bfloat16)
        val = jnp.where(live, r[:, HD:] * inv, 0.0).astype(jnp.bfloat16)
        kbuf[at_rows(u), :] = key
        vbuf[at_rows(u), pl.ds(0, HD)] = val
        cache_ref[at_rows(u), :] = jnp.where(core == 0, key, val)
        return c

    def do_q(u, pair):
        r = project(u, 2 * HD + pair * 2 * HD)
        inv = inv_of(u)
        q = jnp.concatenate(
            [finish(r[:, h * HD:(h + 1) * HD], inv, qg_ref[...], u).astype(jnp.bfloat16) for h in range(2)],
            axis=0,
        )
        rows = rows_of(u, CH, KTILE)
        start = starts_of(rows)
        acc[...] = jnp.zeros_like(acc)

        def one(j, c):
            at = pl.ds(pl.multiple_of(j * KTILE, KTILE), KTILE)
            s = lax.dot_general(
                q, kbuf[at, :], (((1,), (1,)), ((), ())), preferred_element_type=jnp.float32
            )
            keys = j * KTILE + lax.broadcasted_iota(jnp.int32, (CH, KTILE), 1)
            allowed = (keys >= start) & (keys <= rows)
            p = jnp.exp(s * (1.0 / math.sqrt(HD)))
            p = jnp.concatenate(
                [jnp.where(allowed, p[h * CH:(h + 1) * CH], 0.0) for h in range(2)], axis=0
            ).astype(jnp.bfloat16)
            acc[...] += jnp.dot(p, vbuf[at, :], preferred_element_type=jnp.float32)
            return c

        lax.fori_loop(0, u // 2 + 1, one, 0)
        out = (acc[:, :HD] / acc[:, HD:]).astype(jnp.bfloat16)
        for h in range(2):
            ctx_ref[at_rows(u), pl.ds((pair * 2 + h) * HD, HD)] = out[h * CH:(h + 1) * CH]

    def do_q01(u, c):
        do_q(u, 0)
        return c

    def do_q23(u, c):
        do_q(u, 1)
        return c

    def stage(k, lo, hi, fn):
        @pl.when((k >= lo) & (k < hi))
        def _():
            fn(k)

    def tick(k, c):
        stage(k, 0, NCH, a0)
        stage(k, 0, NW, w0)
        stage(k - 2, 0, NCH, a1)
        stage(k - 2, 0, NW, w1)
        stage(k - 3, 0, NCH, a2)
        stage(k - 3, 0, NW, w2)
        stage(k - 4, 0, NCH, a3)
        stage(k - 4, 0, NW, w3)
        stage(k - 5, 0, NCH, a4)
        stage(k - 5, 0, NW, w4)

        @pl.when(k == T_KV)
        def _():
            def ss_wait(j, c):
                ss_msg(lax.rem(t + j, 16), j).wait_recv()
                return c

            lax.fori_loop(1, 16, ss_wait, 0)
            sums = jnp.sum(ss[...], axis=0)
            inv = lax.rsqrt(sums * (1.0 / (8 * FEAT)) + EPS)
            tinv[...] = jnp.transpose(jnp.concatenate([inv] * 8, axis=0))

        last = k - 5
        for first, fn in ((T_KV, do_kv), (T_Q01, do_q01), (T_Q23, do_q23)):
            @pl.when(k >= first)
            def _():
                lax.fori_loop(jnp.where(k == first, 0, last), last + 1, fn, 0)

        return c

    lax.fori_loop(2, NCH + 5, tick, 0)

    swap.wait_send()

    def ss_sent(j, c):
        ss_msg(t, j).wait_send()
        return c

    lax.fori_loop(1, 16, ss_sent, 0)

    def w_sent(i, c):
        w_x(i, g).wait_send()
        for cls in range(2):
            for d in range(2):
                w_z(i, cls, d, g).wait_send()
                w_r(i, cls, d, g).wait_send()
        return c

    lax.fori_loop(0, NW, w_sent, 0)

    def wd_sent(n, c):
        w_d(n // 8, lax.rem(n, 8), core).wait_send()
        return c

    lax.fori_loop(0, 16, wd_sent, 0)

    def a_sent(i, c):
        a_x(i, chip).wait_send()
        for cls in range(2):
            for d in range(2):
                a_y(i, cls, d, chip).wait_send()
                a_r(i, cls, d, chip).wait_send()

        def one(owner, c):
            a_d(i, owner, core).wait_send()
            return c

        lax.fori_loop(0, 8, one, 0)
        return c

    lax.fori_loop(0, NCH, a_sent, 0)


def per_device(activations, norm_gain, query_gain, key_gain, query_weight, keyval_weight, lengths):
    half = np.arange(64, dtype=np.float64)
    freq = np.exp(half * (-2.0 * math.log(THETA) / HD)).astype(np.float32)
    freq = jnp.asarray(np.concatenate([freq, freq])[None, :])
    vmem = pl.BlockSpec(memory_space=pltpu.VMEM)
    hbm = pl.BlockSpec(memory_space=pl.ANY)
    dma = pltpu.SemaphoreType.DMA
    bf16, f32 = jnp.bfloat16, jnp.float32
    sems = []
    for shape in ((NCH,), (NCH, 4), (NCH, 4), (NCH, 8), (NW,), (NW, 4), (NW, 4), (2, 8)):
        sems += [dma(shape), dma(shape)]
    return pl.pallas_call(
        kernel,
        out_shape=(
            jax.ShapeDtypeStruct((ROWS, HD), bf16),
            jax.ShapeDtypeStruct((ROWS, 4 * HD), bf16),
        ),
        in_specs=[pl.BlockSpec(memory_space=pltpu.SMEM)] + [vmem] * 5 + [hbm] * 2,
        out_specs=(vmem, vmem),
        scratch_shapes=[
            pltpu.VMEM((ROWS, 8 * FEAT), bf16),
            pltpu.VMEM((8 * WROWS, 6 * HD), bf16),
            pltpu.VMEM((NCH, HALF, FEAT // 2), bf16),
            pltpu.VMEM((16, 16, CH), f32),
            pltpu.VMEM((CH, CH), f32),
            pltpu.VMEM((CH, CH), f32),
            pltpu.VMEM((ROWS, HD), f32),
            pltpu.VMEM((ROWS, HD), f32),
            pltpu.VMEM((ROWS, HD), bf16),
            pltpu.VMEM((ROWS, 2 * HD), bf16),
            pltpu.VMEM((2 * CH, 2 * HD), f32),
            dma, dma, dma((16,)), dma((16,)), dma((2,)),
            *sems,
        ],
        compiler_params=pltpu.CompilerParams(
            collective_id=0, has_side_effects=True, vmem_limit_bytes=56 * 2**20
        ),
        cost_estimate=pl.CostEstimate(
            flops=2 * ROWS * 5120 * 768, bytes_accessed=4 * 2**20, transcendentals=4 * ROWS * ROWS
        ),
    )(
        lengths,
        activations.reshape(NCH, 2, HALF, FEAT // 2),
        norm_gain[None, :],
        freq,
        query_gain[None, :],
        key_gain[None, :],
        query_weight,
        keyval_weight,
    )


def solution(mesh):
    placed = (P("grp", "tp"), P(), P(), P(), P("grp", "tp"), P("grp", "tp"), P())
    return jax.shard_map(
        per_device,
        mesh=mesh,
        in_specs=placed,
        out_specs=(P("grp", "tp"), P("grp", "tp")),
        check_vma=False,
    )
```

```python
import functools
import math

import jax
import jax.numpy as jnp
import numpy as np
from jax import lax
from jax.experimental import pallas as pl
from jax.experimental.pallas import tpu as pltpu
from jax.sharding import PartitionSpec as P

EPS = 1e-06
THETA = 1000000.0
MESH = pl.DeviceIdType.MESH
HD = 128
ROWS = 1536
CH = 128
HALF = CH // 2
NCH = ROWS // CH
FEAT = 640
WROWS = 640
KH = 320
NW = 10
KTILE = 256
T_KV, T_Q01, T_Q23 = 3, 6, 10
LOG2E = math.log2(math.e)


def kernel(
    len_ref, x_ref, gain_ref, freq_ref, qg_ref, kg_ref, wq_ref, wkv_ref,
    cache_ref, ctx_ref,
    xbuf, nbuf, wbuf, pbuf, ss, ssacc, tinv, cosb, sinb, kbuf, vbuf, cacheb, ctxb,
    out_s, swap_s, swap_r, ss_s, ss_r, loc_s,
    ax_s, ax_r, ay_s, ay_r, ar_s, ar_r, ad_s, ad_r,
    wx_s, wx_r, wz_s, wz_r, wr_s, wr_r, wd_s, wd_r,
):
    g = lax.axis_index("grp")
    t = lax.axis_index("tp")
    core = lax.rem(t, 2)
    chip = t // 2
    xchip = chip + 1 - 2 * lax.rem(chip, 2)

    def chip_of(base, step):
        return lax.rem(base + 2 * step, 8)

    def tp_dev(c, k):
        return (g, c * 2 + k)

    up, down = tp_dev(chip_of(chip, 1), core), tp_dev(chip_of(chip, 3), core)
    across, twin = tp_dev(xchip, core), tp_dev(chip, 1 - core)
    gx = lax.rem(g + 4, 8)

    def ring(base, step):
        return (base // 4) * 4 + lax.rem(lax.rem(base, 4) + step, 4)

    zup, zdown, wacross = (ring(g, 1), t), (ring(g, 3), t), (gx, t)

    bar = pltpu.get_barrier_semaphore()

    def greet(k, c):
        pl.semaphore_signal(bar, inc=1, device_id=(g, lax.rem(t + k, 16)), device_id_type=MESH)
        return c

    lax.fori_loop(1, 16, greet, 0)
    for d in (zup, zdown, wacross):
        pl.semaphore_signal(bar, inc=1, device_id=d, device_id_type=MESH)

    own_w = pl.multiple_of(g * WROWS, WROWS)
    c1 = pltpu.make_async_copy(wq_ref, wbuf.at[pl.ds(own_w, WROWS), pl.ds(2 * HD, 4 * HD)], loc_s.at[0])
    c2 = pltpu.make_async_copy(
        wkv_ref, wbuf.at[pl.ds(own_w, WROWS), pl.ds(pl.multiple_of(core * HD, HD), HD)], loc_s.at[1]
    )
    c1.start()
    c2.start()
    kbuf[...] = jnp.zeros_like(kbuf)
    vbuf[:, :HD] = jnp.zeros((ROWS, HD), jnp.bfloat16)
    vbuf[:, HD:] = jnp.ones((ROWS, HD), jnp.bfloat16)
    ssacc[...] = jnp.zeros_like(ssacc)

    ends = []
    total = 0
    for r in range(8):
        total = total + len_ref[g, r]
        ends.append(total)

    def starts_of(rows):
        start = jnp.zeros_like(rows)
        for r in range(8):
            start = start + jnp.where(rows >= ends[r], len_ref[g, r], 0)
        return start

    def rows_of(u, n, lanes):
        return u * CH + lax.broadcasted_iota(jnp.int32, (n, lanes), 0)

    def trig(u, c):
        rows = rows_of(u, CH, HD)
        angle = (rows - starts_of(rows)).astype(jnp.float32) * freq_ref[...]
        lane = lax.broadcasted_iota(jnp.int32, (CH, HD), 1)
        at = pl.ds(pl.multiple_of(u * CH, CH), CH)
        cosb[at, :] = jnp.cos(angle)
        sinb[at, :] = jnp.where(lane < HD // 2, -1.0, 1.0) * jnp.sin(angle)
        return c

    lax.fori_loop(0, NCH, trig, 0)

    pl.semaphore_wait(bar, 18)

    def rcopy(src, dst, s, r, dev):
        return pltpu.make_async_remote_copy(
            src_ref=src, dst_ref=dst, send_sem=s, recv_sem=r, device_id=dev, device_id_type=MESH
        )

    def swap(i):
        src = x_ref.at[pl.ds(pl.multiple_of(i * CH + (1 - core) * HALF, HALF), HALF), :]
        return rcopy(src, pbuf.at[i], swap_s.at[i], swap_r.at[i], twin)

    def swap_go(i, c):
        swap(i).start()
        return c

    lax.fori_loop(0, NCH, swap_go, 0)

    def wview(owner, i, part=None):
        j = i // 2
        col = pl.multiple_of(jnp.where(j == 0, core * HD, HD + HD * j), HD)
        row = owner * WROWS + lax.rem(i, 2) * KH
        n = KH
        if part is not None:
            n = KH // 2
            row = row + part * n
        return wbuf.at[pl.ds(pl.multiple_of(row, 32), n), pl.ds(col, HD)]

    def wmsg(owner, i, s, r, dev, part=None):
        v = wview(owner, i, part)
        return rcopy(v, v, s, r, dev)

    def w_x(i, owner):
        return wmsg(owner, i, wx_s.at[i], wx_r.at[i], wacross)

    def w_z(i, cls, d, owner):
        k = cls * 2 + d
        return wmsg(owner, i, wz_s.at[i, k], wz_r.at[i, k], (zup, zdown)[d])

    def w_r(i, cls, d, owner):
        k = cls * 2 + d
        return wmsg(owner, i, wr_s.at[i, k], wr_r.at[i, k], (zup, zdown)[d], part=d)

    def kvview(i, slot, col):
        row = slot * WROWS + i * KH
        return wbuf.at[pl.ds(pl.multiple_of(row, 32), KH), pl.ds(pl.multiple_of(col * HD, HD), HD)]

    def w_d(i, owner, col):
        v = kvview(i, owner, col)
        return rcopy(v, v, wd_s.at[i, owner], wd_r.at[i, owner], twin)

    def w_share(i, owner):
        @pl.when(i < 2)
        def _():
            w_d(i, owner, core).start()

    def w_ahead(i):
        w_x(i, g).start()
        w_share(i, g)

    def w0(i):
        w_z(i, 0, 0, g).start()
        w_z(i, 0, 1, g).start()

    def w1(i):
        w_x(i, gx).wait_recv()
        w_z(i, 1, 0, gx).start()
        w_z(i, 1, 1, gx).start()
        w_share(i, gx)

    def w2(i):
        for cls, base in ((0, g), (1, gx)):
            lo, hi = ring(base, 3), ring(base, 1)
            w_z(i, cls, 0, lo).wait_recv()
            w_r(i, cls, 0, lo).start()
            w_share(i, lo)
            w_z(i, cls, 1, hi).wait_recv()
            w_r(i, cls, 1, hi).start()
            w_share(i, hi)

    def w3(i):
        for cls, base in ((0, g), (1, gx)):
            far = ring(base, 2)
            w_r(i, cls, 0, far).wait_recv()
            w_r(i, cls, 1, far).wait_recv()
            w_share(i, far)

    def w4(i):
        @pl.when(i < 2)
        def _():
            def one(owner, c):
                w_d(i, owner, 1 - core).wait_recv()
                return c

            lax.fori_loop(0, 8, one, 0)

    def aview(owner, i, k, part=None):
        row = i * CH + k * HALF
        n = HALF
        if part is not None:
            n = HALF // 2
            row = row + part * n
        return xbuf.at[
            pl.ds(pl.multiple_of(row, 32), n), pl.ds(pl.multiple_of(owner * FEAT, FEAT), FEAT)
        ]

    def amsg(owner, i, s, r, dev, part=None, k=None):
        v = aview(owner, i, core if k is None else k, part)
        return rcopy(v, v, s, r, dev)

    def a_x(i, owner):
        return amsg(owner, i, ax_s.at[i], ax_r.at[i], across)

    def a_y(i, cls, d, owner):
        k = cls * 2 + d
        return amsg(owner, i, ay_s.at[i, k], ay_r.at[i, k], (up, down)[d])

    def a_r(i, cls, d, owner):
        k = cls * 2 + d
        return amsg(owner, i, ar_s.at[i, k], ar_r.at[i, k], (up, down)[d], part=d)

    def a_d(i, owner, k):
        return amsg(owner, i, ad_s.at[i, owner], ad_r.at[i, owner], twin, k=k)

    def a_ahead(i):
        a_x(i, chip).start()
        a_d(i, chip, core).start()

    def a0(i):
        a_y(i, 0, 0, chip).start()
        a_y(i, 0, 1, chip).start()

    def a1(i):
        a_x(i, xchip).wait_recv()
        a_y(i, 1, 0, xchip).start()
        a_y(i, 1, 1, xchip).start()
        a_d(i, xchip, core).start()

    def a2(i):
        for cls, base in ((0, chip), (1, xchip)):
            lo, hi = chip_of(base, 3), chip_of(base, 1)
            a_y(i, cls, 0, lo).wait_recv()
            a_r(i, cls, 0, lo).start()
            a_d(i, lo, core).start()
            a_y(i, cls, 1, hi).wait_recv()
            a_r(i, cls, 1, hi).start()
            a_d(i, hi, core).start()

    def a3(i):
        for cls, base in ((0, chip), (1, xchip)):
            far = chip_of(base, 2)
            a_r(i, cls, 0, far).wait_recv()
            a_r(i, cls, 1, far).wait_recv()
            a_d(i, far, core).start()

    def a4(i):
        def one(owner, c):
            a_d(i, owner, 1 - core).wait_recv()
            return c

        lax.fori_loop(0, 8, one, 0)

    own_f = pl.multiple_of(chip * FEAT, FEAT)

    def merge(i):
        row = pl.multiple_of(i * CH + core * HALF, 32)
        mine = x_ref[pl.ds(row, HALF), :].astype(jnp.float32)
        swap(i).wait_recv()
        other = pbuf[i].astype(jnp.float32)
        first = jnp.where(core == 0, mine, other)
        second = jnp.where(core == 0, other, mine)
        both = jnp.concatenate([first, second], axis=1)
        squares = jnp.sum(both * both, axis=1, keepdims=True)
        xbuf[pl.ds(row, HALF), pl.ds(own_f, FEAT)] = both.astype(jnp.bfloat16)
        lane = lax.broadcasted_iota(jnp.int32, (HALF, CH), 1)
        at = pl.ds(pl.multiple_of(core * HALF, HALF), HALF)
        ssacc[at, :] = jnp.where(lane == i, squares, ssacc[at, :])

    merge(0)
    a_ahead(0)
    a0(0)
    c2.wait()
    c1.wait()
    w_ahead(0)
    w0(0)
    merge(1)
    a_ahead(1)
    merge(2)
    a_ahead(2)
    w_ahead(1)
    w0(1)
    w_ahead(2)
    w_ahead(3)

    def merge_rest(i, c):
        merge(i)
        return c

    lax.fori_loop(3, NCH, merge_rest, 0)
    ss[t] = jnp.transpose(ssacc[...])[:16]

    def ss_msg(slot, k):
        return rcopy(ss.at[slot], ss.at[slot], ss_s.at[k], ss_r.at[slot], (g, lax.rem(t + k, 16)))

    def ss_go(k, c):
        ss_msg(t, k).start()
        return c

    lax.fori_loop(1, 16, ss_go, 0)

    def at_rows(u):
        return pl.ds(pl.multiple_of(u * CH, CH), CH)

    def inv_of(u):
        lane = lax.broadcasted_iota(jnp.int32, (CH, CH), 1)
        return jnp.sum(jnp.where(lane == u, tinv[...], 0.0), axis=1, keepdims=True)

    def finish(a, gains, u):
        m = jnp.mean(a * a, axis=1, keepdims=True)
        a = a * lax.rsqrt(m + EPS) * gains
        return a * cosb[at_rows(u), :] + pltpu.roll(a, HD // 2, 1) * sinb[at_rows(u), :]

    def project(u, col):
        return jnp.dot(
            nbuf[at_rows(u), :], wbuf[:, pl.ds(col, 2 * HD)], preferred_element_type=jnp.float32
        )

    def cache_out(u):
        return pltpu.make_async_copy(cacheb.at[at_rows(u), :], cache_ref.at[at_rows(u), :], out_s.at[u, 2])

    def ctx_out(u, pair):
        cols = pl.ds(pl.multiple_of(pair * 2 * HD, 2 * HD), 2 * HD)
        return pltpu.make_async_copy(ctxb.at[at_rows(u), cols], ctx_ref.at[at_rows(u), cols], out_s.at[u, pair])

    def do_kv(u, c):
        inv = inv_of(u)

        def norm(f, c):
            cols = pl.ds(pl.multiple_of(f * FEAT, FEAT), FEAT)
            x = xbuf[at_rows(u), cols].astype(jnp.float32)
            nbuf[at_rows(u), cols] = (x * inv * gain_ref[:, cols]).astype(jnp.bfloat16)
            return c

        lax.fori_loop(0, 8, norm, 0)
        r = project(u, 0)
        live = rows_of(u, CH, HD) < total
        key = jnp.where(live, finish(r[:, :HD], kg_ref[...], u), 0.0).astype(jnp.bfloat16)
        val = jnp.where(live, r[:, HD:], 0.0).astype(jnp.bfloat16)
        kbuf[at_rows(u), :] = key
        vbuf[at_rows(u), pl.ds(0, HD)] = val
        cacheb[at_rows(u), :] = jnp.where(core == 0, key, val)
        cache_out(u).start()
        return c

    def do_q(u, pair):
        r = project(u, pl.multiple_of(2 * HD + pair * 2 * HD, 2 * HD))
        q = jnp.concatenate(
            [finish(r[:, h * HD:(h + 1) * HD], qg_ref[...], u).astype(jnp.bfloat16) for h in range(2)],
            axis=0,
        )

        def attend(n):
            rows = rows_of(u, CH, n)
            start = starts_of(rows_of(u, CH, HD))[:, :1]
            keys = lax.broadcasted_iota(jnp.int32, (CH, n), 1)
            allowed = (keys >= start) & (keys <= rows)
            s = lax.dot_general(
                q, kbuf[:n, :], (((1,), (1,)), ((), ())), preferred_element_type=jnp.float32
            )
            p = jnp.exp2(s * (LOG2E / math.sqrt(HD)))
            p = jnp.concatenate(
                [jnp.where(allowed, p[h * CH:(h + 1) * CH], 0.0) for h in range(2)], axis=0
            ).astype(jnp.bfloat16)
            a = jnp.dot(p, vbuf[:n, :], preferred_element_type=jnp.float32)
            out = (a[:, :HD] / a[:, HD:]).astype(jnp.bfloat16)
            for h in range(2):
                cols = pl.ds(pl.multiple_of((pair * 2 + h) * HD, HD), HD)
                ctxb[at_rows(u), cols] = out[h * CH:(h + 1) * CH]

        lax.switch(u // 2, [functools.partial(attend, KTILE * (b + 1)) for b in range(ROWS // KTILE)])
        ctx_out(u, pair).start()

    def do_q01(u, c):
        do_q(u, 0)
        return c

    def do_q23(u, c):
        do_q(u, 1)
        return c

    def stage(k, lo, hi, fn):
        @pl.when((k >= lo) & (k < hi))
        def _():
            fn(k)

    def tick(k, c):
        stage(k + 3, 3, NCH, a_ahead)
        stage(k + 1, 1, NCH, a0)
        stage(k + 4, 4, NW, w_ahead)
        stage(k + 2, 2, NW, w0)
        stage(k, 0, NCH, a1)
        stage(k + 1, 1, NW, w1)
        stage(k - 1, 0, NCH, a2)
        stage(k, 0, NW, w2)
        stage(k - 2, 0, NCH, a3)
        stage(k - 1, 0, NW, w3)
        stage(k - 3, 0, NCH, a4)
        stage(k - 2, 0, NW, w4)

        @pl.when(k == T_KV)
        def _():
            def ss_wait(j, c):
                ss_msg(lax.rem(t + j, 16), j).wait_recv()
                return c

            lax.fori_loop(1, 16, ss_wait, 0)
            sums = jnp.sum(ss[...], axis=0)
            inv = lax.rsqrt(sums * (1.0 / (8 * FEAT)) + EPS)
            tinv[...] = jnp.transpose(jnp.concatenate([inv] * 8, axis=0))

        last = k - 3
        for first, fn in ((T_KV, do_kv), (T_Q01, do_q01), (T_Q23, do_q23)):

            @pl.when(k >= first)
            def _():
                lax.fori_loop(jnp.where(k == first, 0, last), last + 1, fn, 0)

        return c

    w1(0)
    lax.fori_loop(0, NCH + 3, tick, 0)

    def ss_sent(j, c):
        ss_msg(t, j).wait_send()
        return c

    lax.fori_loop(1, 16, ss_sent, 0)

    def w_sent(i, c):
        w_x(i, g).wait_send()
        for cls in range(2):
            for d in range(2):
                w_z(i, cls, d, g).wait_send()
                w_r(i, cls, d, g).wait_send()
        return c

    lax.fori_loop(0, NW, w_sent, 0)

    def wd_sent(n, c):
        w_d(n // 8, lax.rem(n, 8), core).wait_send()
        return c

    lax.fori_loop(0, 16, wd_sent, 0)

    def a_sent(i, c):
        a_x(i, chip).wait_send()
        for cls in range(2):
            for d in range(2):
                a_y(i, cls, d, chip).wait_send()
                a_r(i, cls, d, chip).wait_send()

        def one(owner, c):
            a_d(i, owner, core).wait_send()
            return c

        lax.fori_loop(0, 8, one, 0)
        swap(i).wait_send()
        cache_out(i).wait()
        ctx_out(i, 0).wait()
        ctx_out(i, 1).wait()
        return c

    lax.fori_loop(0, NCH, a_sent, 0)


def hand_on(cache_in, ctx_in, cache_ref, ctx_ref, sem):
    part = ROWS // 4
    copies = []
    for n in range(4):
        rows = pl.ds(n * part, part)
        copies.append(pltpu.make_async_copy(cache_in.at[rows, :], cache_ref.at[rows, :], sem.at[2 * n]))
        copies.append(pltpu.make_async_copy(ctx_in.at[rows, :], ctx_ref.at[rows, :], sem.at[2 * n + 1]))
    for c in copies:
        c.start()
    for c in copies:
        c.wait()


def per_device(activations, norm_gain, query_gain, key_gain, query_weight, keyval_weight, lengths):
    half = np.arange(64, dtype=np.float64)
    freq = np.exp(half * (-2.0 * math.log(THETA) / HD)).astype(np.float32)
    freq = jnp.asarray(np.concatenate([freq, freq])[None, :])
    vmem = pl.BlockSpec(memory_space=pltpu.VMEM)
    hbm = pl.BlockSpec(memory_space=pl.ANY)
    dma = pltpu.SemaphoreType.DMA
    bf16, f32 = jnp.bfloat16, jnp.float32
    sems = []
    for shape in ((NCH,), (NCH, 4), (NCH, 4), (NCH, 8), (NW,), (NW, 4), (NW, 4), (2, 8)):
        sems += [dma(shape), dma(shape)]
    cache, context = pl.pallas_call(
        kernel,
        out_shape=(
            jax.ShapeDtypeStruct((ROWS, HD), bf16),
            jax.ShapeDtypeStruct((ROWS, 4 * HD), bf16),
        ),
        in_specs=[pl.BlockSpec(memory_space=pltpu.SMEM)] + [vmem] * 5 + [hbm] * 2,
        out_specs=(hbm, hbm),
        scratch_shapes=[
            pltpu.VMEM((ROWS, 8 * FEAT), bf16),
            pltpu.VMEM((ROWS, 8 * FEAT), bf16),
            pltpu.VMEM((8 * WROWS, 6 * HD), bf16),
            pltpu.VMEM((NCH, HALF, FEAT // 2), bf16),
            pltpu.VMEM((16, 16, CH), f32),
            pltpu.VMEM((CH, CH), f32),
            pltpu.VMEM((CH, CH), f32),
            pltpu.VMEM((ROWS, HD), f32),
            pltpu.VMEM((ROWS, HD), f32),
            pltpu.VMEM((ROWS, HD), bf16),
            pltpu.VMEM((ROWS, 2 * HD), bf16),
            pltpu.VMEM((ROWS, HD), bf16),
            pltpu.VMEM((ROWS, 4 * HD), bf16),
            dma((NCH, 3)), dma((NCH,)), dma((NCH,)), dma((16,)), dma((16,)), dma((2,)),
            *sems,
        ],
        compiler_params=pltpu.CompilerParams(
            collective_id=0, has_side_effects=True, vmem_limit_bytes=56 * 2**20
        ),
        cost_estimate=pl.CostEstimate(
            flops=2 * ROWS * 5120 * 768, bytes_accessed=4 * 2**20, transcendentals=4 * ROWS * ROWS
        ),
    )(
        lengths,
        activations,
        norm_gain[None, :],
        freq,
        query_gain[None, :],
        key_gain[None, :],
        query_weight,
        keyval_weight,
    )
    return pl.pallas_call(
        hand_on,
        out_shape=(
            jax.ShapeDtypeStruct((ROWS, HD), bf16),
            jax.ShapeDtypeStruct((ROWS, 4 * HD), bf16),
        ),
        in_specs=[hbm] * 2,
        out_specs=(hbm, hbm),
        scratch_shapes=[dma((8,))],
    )(cache, context)


def solution(mesh):
    placed = (P("grp", "tp"), P(), P(), P(), P("grp", "tp"), P("grp", "tp"), P())
    return jax.shard_map(
        per_device,
        mesh=mesh,
        in_specs=placed,
        out_specs=(P("grp", "tp"), P("grp", "tp")),
        check_vma=False,
    )
```

```python
import functools
import math

import jax
import jax.numpy as jnp
import numpy as np
from jax import lax
from jax.experimental import pallas as pl
from jax.experimental.pallas import tpu as pltpu
from jax.sharding import PartitionSpec as P

EPS = 1e-06
THETA = 1000000.0
MESH = pl.DeviceIdType.MESH
HD = 128
ROWS = 1536
CH = 128
NCH = ROWS // CH
FEAT = 320
WROWS = 640
KH = 320
NW = 10
KTILE = 256
T_KV, T_Q01, T_Q23 = 3, 5, 8
LEAD = 3
LOG2E = math.log2(math.e)


def kernel(
    len_ref, x_ref, gain_ref, freq_ref, qg_ref, kg_ref, wq_ref, wkv_ref,
    cache_ref, ctx_ref,
    xbuf, nbuf, wbuf, gcol, ss, tinv, cosb, sinb, kbuf, vbuf, cacheb, ctxb,
    out_s, ss_s, ss_r, loc_s, a_s, a_r, w_s, w_r,
):
    g = lax.axis_index("grp")
    t = lax.axis_index("tp")
    core = lax.rem(t, 2)
    chip = t // 2
    xchip = chip + 1 - 2 * lax.rem(chip, 2)

    def chip_of(base, step):
        return lax.rem(base + 2 * step, 8)

    def tp_dev(c, k):
        return (g, c * 2 + k)

    up, down = tp_dev(chip_of(chip, 1), core), tp_dev(chip_of(chip, 3), core)
    across, twin = tp_dev(xchip, core), tp_dev(chip, 1 - core)
    gx = lax.rem(g + 4, 8)

    def ring(base, step):
        return (base // 4) * 4 + lax.rem(lax.rem(base, 4) + step, 4)

    zup, zdown, wacross = (ring(g, 1), t), (ring(g, 3), t), (gx, t)

    bar = pltpu.get_barrier_semaphore()

    def greet(k, c):
        pl.semaphore_signal(bar, inc=1, device_id=(g, lax.rem(t + k, 16)), device_id_type=MESH)
        return c

    lax.fori_loop(1, 16, greet, 0)
    for d in (zup, zdown, wacross):
        pl.semaphore_signal(bar, inc=1, device_id=d, device_id_type=MESH)

    own_w = pl.multiple_of(g * WROWS, WROWS)
    c1 = pltpu.make_async_copy(wq_ref, wbuf.at[pl.ds(own_w, WROWS), pl.ds(2 * HD, 4 * HD)], loc_s.at[0])
    c2 = pltpu.make_async_copy(
        wkv_ref, wbuf.at[pl.ds(own_w, WROWS), pl.ds(pl.multiple_of(core * HD, HD), HD)], loc_s.at[1]
    )
    c1.start()
    c2.start()
    own_f = pl.multiple_of(t * FEAT, FEAT)
    ss[t] = jnp.zeros((16, CH), jnp.float32)

    def stage_own(i, c):
        cols = pl.ds(pl.multiple_of(i * CH, CH), CH)
        mine = x_ref[:, cols]
        xbuf[pl.ds(own_f, FEAT), cols] = mine
        mine = mine.astype(jnp.float32)
        ss[t, pl.ds(i, 1), :] = jnp.sum(mine * mine, axis=0, keepdims=True)
        return c

    lax.fori_loop(0, NCH, stage_own, 0)


    ends = []
    total = 0
    for r in range(8):
        total = total + len_ref[g, r]
        ends.append(total)

    def starts_of(rows):
        start = jnp.zeros_like(rows)
        for r in range(8):
            start = start + jnp.where(rows >= ends[r], len_ref[g, r], 0)
        return start

    def rows_of(u, n, lanes):
        return u * CH + lax.broadcasted_iota(jnp.int32, (n, lanes), 0)

    def trig(u, c):
        rows = rows_of(u, CH, HD)
        angle = (rows - starts_of(rows)).astype(jnp.float32) * freq_ref[...]
        lane = lax.broadcasted_iota(jnp.int32, (CH, HD), 1)
        at = pl.ds(pl.multiple_of(u * CH, CH), CH)
        cosb[at, :] = jnp.cos(angle)
        sinb[at, :] = jnp.where(lane < HD // 2, -1.0, 1.0) * jnp.sin(angle)
        return c


    def gain_column(f, c):
        at = pl.ds(pl.multiple_of(f * HD, HD), HD)
        gcol[at, :] = jnp.transpose(jnp.broadcast_to(gain_ref[:, at], (HD, HD)))
        return c

    pl.semaphore_wait(bar, 18)

    def rcopy(src, dst, s, r, dev):
        return pltpu.make_async_remote_copy(
            src_ref=src, dst_ref=dst, send_sem=s, recv_sem=r, device_id=dev, device_id_type=MESH
        )

    def wview(owner, i, part=None):
        j = i // 2
        col = pl.multiple_of(jnp.where(j == 0, core * HD, HD + HD * j), HD)
        row = owner * WROWS + lax.rem(i, 2) * KH
        n = KH
        if part is not None:
            n = KH // 2
            row = row + part * n
        return wbuf.at[pl.ds(pl.multiple_of(row, 32), n), pl.ds(col, HD)]

    def wmsg(owner, i, s, r, dev, part=None):
        v = wview(owner, i, part)
        return rcopy(v, v, s, r, dev)

    def w_x(i, owner):
        return wmsg(owner, i, w_s.at[i], w_r.at[i, 0], wacross)

    def w_z(i, cls, d, owner):
        return wmsg(owner, i, w_s.at[i], w_r.at[i, 1 + cls], (zup, zdown)[d])

    def w_r_(i, cls, d, owner):
        return wmsg(owner, i, w_s.at[i], w_r.at[i, 3 + cls], (zup, zdown)[d], part=d)

    def w_got(i, k, n):
        v = wbuf.at[pl.ds(0, n * KH), pl.ds(0, HD)]
        rcopy(v, v, w_s.at[i], w_r.at[i, k], wacross).wait_recv()

    def kvview(i, slot, col):
        row = slot * WROWS + i * KH
        return wbuf.at[pl.ds(pl.multiple_of(row, 32), KH), pl.ds(pl.multiple_of(col * HD, HD), HD)]

    def w_d(i, owner, col):
        v = kvview(i, owner, col)
        return rcopy(v, v, w_s.at[i], w_r.at[i, 5], twin)

    def w_share(i, owner):
        @pl.when(i < 2)
        def _():
            w_d(i, owner, core).start()

    def w_ahead(i):
        w_x(i, g).start()
        w_share(i, g)

    def w0(i):
        w_z(i, 0, 0, g).start()
        w_z(i, 0, 1, g).start()

    def mixed(i):
        return (i >= 2) & (lax.rem(i, 2) == 0)

    def w_f(i, n, owner):
        return wmsg(owner, i, w_s.at[i], w_r.at[i, (2, 2, 4)[n]], wacross)

    def w1(i):
        w_got(i, 0, 1)

        @pl.when(jnp.logical_not(mixed(i)))
        def _():
            w_z(i, 1, 0, gx).start()
            w_z(i, 1, 1, gx).start()

        w_share(i, gx)

    def w2(i):
        def near(cls, base):
            lo, hi = ring(base, 3), ring(base, 1)
            w_got(i, 1 + cls, 2)
            w_r_(i, cls, 0, lo).start()
            w_r_(i, cls, 1, hi).start()
            w_share(i, lo)
            w_share(i, hi)

        near(0, g)

        @pl.when(mixed(i))
        def _():
            w_f(i, 0, ring(g, 3)).start()
            w_f(i, 1, ring(g, 1)).start()

        @pl.when(jnp.logical_not(mixed(i)))
        def _():
            near(1, gx)

    def w3(i):
        w_got(i, 3, 1)
        w_share(i, ring(g, 2))

        @pl.when(mixed(i))
        def _():
            w_f(i, 2, ring(g, 2)).start()

        @pl.when(jnp.logical_not(mixed(i)))
        def _():
            w_got(i, 4, 1)
            w_share(i, ring(gx, 2))

    def w4(i):
        @pl.when(i < 2)
        def _():
            w_got(i, 5, 8)

        @pl.when(mixed(i))
        def _():
            w_got(i, 2, 2)
            w_got(i, 4, 1)

    def aview(owner, i, k, part=None):
        row = (owner * 2 + k) * FEAT
        n = FEAT
        if part is not None:
            n = FEAT // 2
            row = row + part * n
        return xbuf.at[pl.ds(pl.multiple_of(row, 32), n), pl.ds(pl.multiple_of(i * CH, CH), CH)]

    def amsg(owner, i, s, r, dev, part=None, k=None):
        v = aview(owner, i, core if k is None else k, part)
        return rcopy(v, v, s, r, dev)

    def a_x(i, owner):
        return amsg(owner, i, a_s.at[i], a_r.at[i, 0], across)

    def a_y(i, cls, d, owner):
        return amsg(owner, i, a_s.at[i], a_r.at[i, 1 + cls], (up, down)[d])

    def a_r_(i, cls, d, owner):
        return amsg(owner, i, a_s.at[i], a_r.at[i, 3 + cls], (up, down)[d], part=d)

    def a_d(i, owner, k):
        return amsg(owner, i, a_s.at[i], a_r.at[i, 5], twin, k=k)

    def a_got(i, k, n):
        v = xbuf.at[pl.ds(0, n * FEAT), pl.ds(0, CH)]
        rcopy(v, v, a_s.at[i], a_r.at[i, k], across).wait_recv()

    def a_ahead(i):
        a_x(i, chip).start()
        a_d(i, chip, core).start()

    def a0(i):
        a_y(i, 0, 0, chip).start()
        a_y(i, 0, 1, chip).start()

    def a1(i):
        a_got(i, 0, 1)
        a_y(i, 1, 0, xchip).start()
        a_y(i, 1, 1, xchip).start()
        a_d(i, xchip, core).start()

    def a2(i):
        for cls, base in ((0, chip), (1, xchip)):
            lo, hi = chip_of(base, 3), chip_of(base, 1)
            a_got(i, 1 + cls, 2)
            a_r_(i, cls, 0, lo).start()
            a_r_(i, cls, 1, hi).start()
            a_d(i, lo, core).start()
            a_d(i, hi, core).start()

    def a3(i):
        for cls, base in ((0, chip), (1, xchip)):
            a_got(i, 3 + cls, 1)
            a_d(i, chip_of(base, 2), core).start()

    def a4(i):
        a_got(i, 5, 8)

    for i in range(LEAD):
        a0(i)
        a_ahead(i)
    c2.wait()
    c1.wait()
    for i in range(LEAD):
        w_ahead(i)
        w0(i)

    def ss_msg(slot, k):
        return rcopy(ss.at[slot], ss.at[slot], ss_s, ss_r, (g, lax.rem(t + k, 16)))

    def ss_go(k, c):
        ss_msg(t, k).start()
        return c

    lax.fori_loop(1, 16, ss_go, 0)

    def at_rows(u):
        return pl.ds(pl.multiple_of(u * CH, CH), CH)

    def finish(a, gains, u):
        m = jnp.mean(a * a, axis=1, keepdims=True)
        a = a * lax.rsqrt(m + EPS) * gains
        return a * cosb[at_rows(u), :] + pltpu.roll(a, HD // 2, 1) * sinb[at_rows(u), :]

    def project(u, col):
        return lax.dot_general(
            nbuf[:, at_rows(u)],
            wbuf[:, pl.ds(col, 2 * HD)],
            (((0,), (0,)), ((), ())),
            preferred_element_type=jnp.float32,
        )

    def cache_out(u):
        return pltpu.make_async_copy(cacheb.at[at_rows(u), :], cache_ref.at[at_rows(u), :], out_s.at[0])

    def ctx_out(u, pair):
        cols = pl.ds(pl.multiple_of(pair * 2 * HD, 2 * HD), 2 * HD)
        return pltpu.make_async_copy(ctxb.at[at_rows(u), cols], ctx_ref.at[at_rows(u), cols], out_s.at[1])

    def do_kv(u, c):
        inv = tinv[pl.ds(u, 1), :]

        def norm(f, c):
            rows = pl.ds(pl.multiple_of(f * 2 * FEAT, 2 * FEAT), 2 * FEAT)
            x = xbuf[rows, at_rows(u)].astype(jnp.float32)
            nbuf[rows, at_rows(u)] = (x * inv * gcol[rows, :]).astype(jnp.bfloat16)
            return c

        lax.fori_loop(0, 8, norm, 0)
        r = project(u, 0)
        live = rows_of(u, CH, HD) < total
        key = jnp.where(live, finish(r[:, :HD], kg_ref[...], u), 0.0).astype(jnp.bfloat16)
        val = jnp.where(live, r[:, HD:], 0.0).astype(jnp.bfloat16)
        kbuf[at_rows(u), :] = key
        vbuf[at_rows(u), pl.ds(0, HD)] = val
        cacheb[at_rows(u), :] = jnp.where(core == 0, key, val)
        cache_out(u).start()
        return c

    def do_q(u, pair):
        r = project(u, pl.multiple_of(2 * HD + pair * 2 * HD, 2 * HD))
        q = jnp.concatenate(
            [finish(r[:, h * HD:(h + 1) * HD], qg_ref[...], u).astype(jnp.bfloat16) for h in range(2)],
            axis=0,
        )

        def attend(n):
            rows = rows_of(u, CH, n)
            start = starts_of(rows_of(u, CH, HD))[:, :1]
            keys = lax.broadcasted_iota(jnp.int32, (CH, n), 1)
            allowed = (keys >= start) & (keys <= rows)
            s = lax.dot_general(
                q, kbuf[:n, :], (((1,), (1,)), ((), ())), preferred_element_type=jnp.float32
            )
            p = jnp.exp2(s * (LOG2E / math.sqrt(HD)))
            p = jnp.concatenate(
                [jnp.where(allowed, p[h * CH:(h + 1) * CH], 0.0) for h in range(2)], axis=0
            ).astype(jnp.bfloat16)
            a = jnp.dot(p, vbuf[:n, :], preferred_element_type=jnp.float32)
            out = (a[:, :HD] / a[:, HD:]).astype(jnp.bfloat16)
            for h in range(2):
                cols = pl.ds(pl.multiple_of((pair * 2 + h) * HD, HD), HD)
                ctxb[at_rows(u), cols] = out[h * CH:(h + 1) * CH]

        lax.switch(u // 2, [functools.partial(attend, KTILE * (b + 1)) for b in range(ROWS // KTILE)])
        ctx_out(u, pair).start()

    def do_q01(u, c):
        do_q(u, 0)
        return c

    def do_q23(u, c):
        do_q(u, 1)
        return c

    def stage(k, lo, hi, fn):
        @pl.when((k >= lo) & (k < hi))
        def _():
            fn(k)

    def w_step(k):
        stage(k + LEAD, LEAD, NW, w_ahead)
        stage(k + LEAD, LEAD, NW, w0)
        stage(k, 0, NW, w1)
        stage(k - 1, 0, NW, w2)
        stage(k - 2, 0, NW, w3)
        stage(k - 3, 0, NW, w4)

    def tick(k, c):
        stage(k + LEAD, LEAD, NCH, a_ahead)
        stage(k + LEAD, LEAD, NCH, a0)
        stage(k, 0, NCH, a1)
        stage(k - 1, 0, NCH, a2)
        stage(k - 2, 0, NCH, a3)
        first_step = k + (k + 3) // 4
        w_step(first_step)

        @pl.when(lax.rem(k, 4) == 0)
        def _():
            w_step(first_step + 1)

        stage(k - 3, 0, NCH, a4)

        @pl.when(k == 0)
        def _():
            kbuf[...] = jnp.zeros_like(kbuf)
            vbuf[:, :HD] = jnp.zeros((ROWS, HD), jnp.bfloat16)
            vbuf[:, HD:] = jnp.ones((ROWS, HD), jnp.bfloat16)

        @pl.when(k == 1)
        def _():
            lax.fori_loop(0, 16 * FEAT // HD, gain_column, 0)

        @pl.when(k < NCH)
        def _():
            trig(k, 0)

        @pl.when(k == T_KV)
        def _():
            v = ss.at[pl.ds(0, 15)]
            rcopy(v, v, ss_s, ss_r, twin).wait_recv()
            sums = jnp.sum(ss[...], axis=0)
            tinv[...] = lax.rsqrt(sums * (1.0 / (16 * FEAT)) + EPS)

        last = k - 3
        for first, fn in ((T_KV, do_kv), (T_Q01, do_q01), (T_Q23, do_q23)):

            @pl.when(k >= first)
            def _():
                lax.fori_loop(jnp.where(k == first, 0, last), last + 1, fn, 0)

        return c

    lax.fori_loop(0, NCH + 3, tick, 0)

    v = ss.at[pl.ds(0, 15)]
    rcopy(v, v, ss_s, ss_r, twin).wait_send()

    def w_sent(i, c):
        v = wbuf.at[pl.ds(0, 7 * KH), pl.ds(0, HD)]
        rcopy(v, v, w_s.at[i], w_r.at[i, 0], twin).wait_send()

        return c

    def kv_sent(i, c):
        v = wbuf.at[pl.ds(0, 15 * KH), pl.ds(0, HD)]
        rcopy(v, v, w_s.at[i], w_r.at[i, 0], twin).wait_send()
        return c

    lax.fori_loop(0, 2, kv_sent, 0)
    lax.fori_loop(2, NW, w_sent, 0)

    def a_sent(i, c):
        v = xbuf.at[pl.ds(0, 15 * FEAT), pl.ds(0, CH)]
        rcopy(v, v, a_s.at[i], a_r.at[i, 0], twin).wait_send()
        return c

    lax.fori_loop(0, NCH, a_sent, 0)
    pltpu.make_async_copy(cacheb, cache_ref, out_s.at[0]).wait()
    pltpu.make_async_copy(ctxb, ctx_ref, out_s.at[1]).wait()


def hand_on(cache_in, ctx_in, cache_ref, ctx_ref, cache_held, ctx_held, sem):
    parts = []
    for n in range(4):
        rows = pl.ds(n * ROWS // 4, ROWS // 4)
        for a, (src, held, dst) in enumerate(((cache_in, cache_held, cache_ref), (ctx_in, ctx_held, ctx_ref))):
            parts.append(
                (
                    pltpu.make_async_copy(src.at[rows, :], held.at[rows, :], sem.at[n, a, 0]),
                    pltpu.make_async_copy(held.at[rows, :], dst.at[rows, :], sem.at[n, a, 1]),
                )
            )
    for fetch, _ in parts:
        fetch.start()
    for fetch, store in parts:
        fetch.wait()
        store.start()
    for _, store in parts:
        store.wait()


def per_device(activations, norm_gain, query_gain, key_gain, query_weight, keyval_weight, lengths):
    half = np.arange(64, dtype=np.float64)
    freq = np.exp(half * (-2.0 * math.log(THETA) / HD)).astype(np.float32)
    freq = jnp.asarray(np.concatenate([freq, freq])[None, :])
    vmem = pl.BlockSpec(memory_space=pltpu.VMEM)
    hbm = pl.BlockSpec(memory_space=pl.ANY)
    dma = pltpu.SemaphoreType.DMA
    bf16, f32 = jnp.bfloat16, jnp.float32
    cache, context = pl.pallas_call(
        kernel,
        out_shape=(
            jax.ShapeDtypeStruct((ROWS, HD), bf16),
            jax.ShapeDtypeStruct((ROWS, 4 * HD), bf16),
        ),
        in_specs=[pl.BlockSpec(memory_space=pltpu.SMEM)] + [vmem] * 5 + [hbm] * 2,
        out_specs=(hbm, hbm),
        scratch_shapes=[
            pltpu.VMEM((16 * FEAT, ROWS), bf16),
            pltpu.VMEM((16 * FEAT, ROWS), bf16),
            pltpu.VMEM((8 * WROWS, 6 * HD), bf16),
            pltpu.VMEM((16 * FEAT, HD), f32),
            pltpu.VMEM((16, 16, CH), f32),
            pltpu.VMEM((16, CH), f32),
            pltpu.VMEM((ROWS, HD), f32),
            pltpu.VMEM((ROWS, HD), f32),
            pltpu.VMEM((ROWS, HD), bf16),
            pltpu.VMEM((ROWS, 2 * HD), bf16),
            pltpu.VMEM((ROWS, HD), bf16),
            pltpu.VMEM((ROWS, 4 * HD), bf16),
            dma((2,)), dma, dma, dma((2,)),
            dma((NCH,)), dma((NCH, 6)), dma((NW,)), dma((NW, 6)),
        ],
        compiler_params=pltpu.CompilerParams(
            collective_id=0, has_side_effects=True, vmem_limit_bytes=56 * 2**20
        ),
        cost_estimate=pl.CostEstimate(
            flops=2 * ROWS * 5120 * 768, bytes_accessed=4 * 2**20, transcendentals=4 * ROWS * ROWS
        ),
    )(
        lengths,
        activations.T,
        norm_gain[None, :],
        freq,
        query_gain[None, :],
        key_gain[None, :],
        query_weight,
        keyval_weight,
    )
    return pl.pallas_call(
        hand_on,
        out_shape=(
            jax.ShapeDtypeStruct((ROWS, HD), bf16),
            jax.ShapeDtypeStruct((ROWS, 4 * HD), bf16),
        ),
        in_specs=[hbm] * 2,
        out_specs=(hbm, hbm),
        scratch_shapes=[
            pltpu.VMEM((ROWS, HD), bf16),
            pltpu.VMEM((ROWS, 4 * HD), bf16),
            dma((4, 2, 2)),
        ],
        compiler_params=pltpu.CompilerParams(vmem_limit_bytes=60 * 2**20),
    )(cache, context)


def solution(mesh):
    placed = (P("grp", "tp"), P(), P(), P(), P("grp", "tp"), P("grp", "tp"), P())
    return jax.shard_map(
        per_device,
        mesh=mesh,
        in_specs=placed,
        out_specs=(P("grp", "tp"), P("grp", "tp")),
        check_vma=False,
    )
```

```python
import functools
import math

import jax
import jax.numpy as jnp
import numpy as np
from jax import lax
from jax.experimental import pallas as pl
from jax.experimental.pallas import tpu as pltpu
from jax.sharding import PartitionSpec as P

EPS = 1e-06
THETA = 1000000.0
MESH = pl.DeviceIdType.MESH
HD = 128
ROWS = 1536
CH = 128
NCH = ROWS // CH
FEAT = 320
WROWS = 640
KH = 320
NW = 10
KTILE = 256
LAG = 5
UNIT = 2 * CH
TASKS = (
    (8, 0, 0), (9, 0, 1), (10, 0, 2), (12, 0, 3), (12, 1, 0), (12, 1, 1), (13, 1, 2), (13, 1, 3),
    (14, 0, 4), (15, 1, 4), (16, 0, 5), (16, 1, 5),
)
LEAD = 3
LOG2E = math.log2(math.e)


def kernel(
    len_ref, x_ref, gain_ref, freq_ref, qg_ref, kg_ref, wq_ref, wkv_ref,
    cache_ref, ctx_ref,
    xbuf, nbuf, wbuf, gcol, ss, tinv, cosb, sinb, kbuf, vbuf, cacheb, ctxb,
    out_s, ss_s, ss_r, loc_s, a_s, a_r, w_s, w_r,
):
    g = lax.axis_index("grp")
    t = lax.axis_index("tp")
    core = lax.rem(t, 2)
    chip = t // 2
    xchip = chip + 1 - 2 * lax.rem(chip, 2)

    def chip_of(base, step):
        return lax.rem(base + 2 * step, 8)

    def tp_dev(c, k):
        return (g, c * 2 + k)

    up, down = tp_dev(chip_of(chip, 1), core), tp_dev(chip_of(chip, 3), core)
    across, twin = tp_dev(xchip, core), tp_dev(chip, 1 - core)
    gx = lax.rem(g + 4, 8)

    def ring(base, step):
        return (base // 4) * 4 + lax.rem(lax.rem(base, 4) + step, 4)

    zup, zdown, wacross = (ring(g, 1), t), (ring(g, 3), t), (gx, t)

    bar = pltpu.get_barrier_semaphore()

    def greet(k, c):
        pl.semaphore_signal(bar, inc=1, device_id=(g, lax.rem(t + k, 16)), device_id_type=MESH)
        return c

    lax.fori_loop(1, 16, greet, 0)
    for d in (zup, zdown, wacross):
        pl.semaphore_signal(bar, inc=1, device_id=d, device_id_type=MESH)

    own_w = pl.multiple_of(g * WROWS, WROWS)
    c1 = pltpu.make_async_copy(wq_ref, wbuf.at[pl.ds(own_w, WROWS), pl.ds(2 * HD, 4 * HD)], loc_s.at[0])
    c2 = pltpu.make_async_copy(
        wkv_ref, wbuf.at[pl.ds(own_w, WROWS), pl.ds(pl.multiple_of(core * HD, HD), HD)], loc_s.at[1]
    )
    c1.start()
    c2.start()
    own_f = pl.multiple_of(t * FEAT, FEAT)
    ss[t] = jnp.zeros((16, CH), jnp.float32)

    def stage_own(i, c):
        cols = pl.ds(pl.multiple_of(i * CH, CH), CH)
        mine = x_ref[:, cols]
        xbuf[pl.ds(own_f, FEAT), cols] = mine
        mine = mine.astype(jnp.float32)
        ss[t, pl.ds(i, 1), :] = jnp.sum(mine * mine, axis=0, keepdims=True)
        return c

    lax.fori_loop(0, NCH, stage_own, 0)


    ends = []
    total = 0
    for r in range(8):
        total = total + len_ref[g, r]
        ends.append(total)

    def starts_of(rows):
        start = jnp.zeros_like(rows)
        for r in range(8):
            start = start + jnp.where(rows >= ends[r], len_ref[g, r], 0)
        return start

    def rows_of(u, n, lanes):
        return u * CH + lax.broadcasted_iota(jnp.int32, (n, lanes), 0)

    def trig(u, c):
        rows = rows_of(u, CH, HD)
        angle = (rows - starts_of(rows)).astype(jnp.float32) * freq_ref[...]
        lane = lax.broadcasted_iota(jnp.int32, (CH, HD), 1)
        at = pl.ds(pl.multiple_of(u * CH, CH), CH)
        cosb[at, :] = jnp.cos(angle)
        sinb[at, :] = jnp.where(lane < HD // 2, -1.0, 1.0) * jnp.sin(angle)
        return c


    def gain_column(f, c):
        at = pl.ds(pl.multiple_of(f * HD, HD), HD)
        gcol[at, :] = jnp.transpose(jnp.broadcast_to(gain_ref[:, at], (HD, HD)))
        return c

    pl.semaphore_wait(bar, 18)

    def rcopy(src, dst, s, r, dev):
        return pltpu.make_async_remote_copy(
            src_ref=src, dst_ref=dst, send_sem=s, recv_sem=r, device_id=dev, device_id_type=MESH
        )

    def wview(owner, i, part=None):
        j = i // 2
        col = pl.multiple_of(jnp.where(j == 0, core * HD, HD + HD * j), HD)
        row = owner * WROWS + lax.rem(i, 2) * KH
        n = KH
        if part is not None:
            n = KH // 2
            row = row + part * n
        return wbuf.at[pl.ds(pl.multiple_of(row, 32), n), pl.ds(col, HD)]

    def wmsg(owner, i, s, r, dev, part=None):
        v = wview(owner, i, part)
        return rcopy(v, v, s, r, dev)

    def w_x(i, owner):
        return wmsg(owner, i, w_s.at[i], w_r.at[i, 0], wacross)

    def w_z(i, cls, d, owner):
        return wmsg(owner, i, w_s.at[i], w_r.at[i, 1 + cls], (zup, zdown)[d])

    def w_r_(i, cls, d, owner):
        return wmsg(owner, i, w_s.at[i], w_r.at[i, 3 + cls], (zup, zdown)[d], part=d)

    def w_got(i, k, n):
        v = wbuf.at[pl.ds(0, n * KH), pl.ds(0, HD)]
        rcopy(v, v, w_s.at[i], w_r.at[i, k], wacross).wait_recv()

    def kvview(i, slot, col):
        row = slot * WROWS + i * KH
        return wbuf.at[pl.ds(pl.multiple_of(row, 32), KH), pl.ds(pl.multiple_of(col * HD, HD), HD)]

    def w_d(i, owner, col):
        v = kvview(i, owner, col)
        return rcopy(v, v, w_s.at[i], w_r.at[i, 5], twin)

    def w_share(i, owner):
        @pl.when(i < 2)
        def _():
            w_d(i, owner, core).start()

    def w_ahead(i):
        w_x(i, g).start()
        w_share(i, g)

    def w0(i):
        w_z(i, 0, 0, g).start()
        w_z(i, 0, 1, g).start()

    def mixed(i):
        return i < 0

    def w_f(i, n, owner):
        return wmsg(owner, i, w_s.at[i], w_r.at[i, (2, 2, 4)[n]], wacross)

    def w1(i):
        w_got(i, 0, 1)

        @pl.when(jnp.logical_not(mixed(i)))
        def _():
            w_z(i, 1, 0, gx).start()
            w_z(i, 1, 1, gx).start()

        w_share(i, gx)

    def w2(i):
        def near(cls, base):
            lo, hi = ring(base, 3), ring(base, 1)
            w_got(i, 1 + cls, 2)
            w_r_(i, cls, 0, lo).start()
            w_r_(i, cls, 1, hi).start()
            w_share(i, lo)
            w_share(i, hi)

        near(0, g)

        @pl.when(mixed(i))
        def _():
            w_f(i, 0, ring(g, 3)).start()
            w_f(i, 1, ring(g, 1)).start()

        @pl.when(jnp.logical_not(mixed(i)))
        def _():
            near(1, gx)

    def w3(i):
        w_got(i, 3, 1)
        w_share(i, ring(g, 2))

        @pl.when(mixed(i))
        def _():
            w_f(i, 2, ring(g, 2)).start()

        @pl.when(jnp.logical_not(mixed(i)))
        def _():
            w_got(i, 4, 1)
            w_share(i, ring(gx, 2))

    def w4(i):
        @pl.when(i < 2)
        def _():
            w_got(i, 5, 8)

        @pl.when(mixed(i))
        def _():
            w_got(i, 2, 2)
            w_got(i, 4, 1)

    def aview(owner, i, k, part=None):
        row = (owner * 2 + k) * FEAT
        n = FEAT
        if part is not None:
            n = FEAT // 2
            row = row + part * n
        return xbuf.at[pl.ds(pl.multiple_of(row, 32), n), pl.ds(pl.multiple_of(i * CH, CH), CH)]

    def amsg(owner, i, s, r, dev, part=None, k=None):
        v = aview(owner, i, core if k is None else k, part)
        return rcopy(v, v, s, r, dev)

    def a_x(i, owner):
        return amsg(owner, i, a_s.at[i], a_r.at[i, 0], across)

    def a_y(i, cls, d, owner):
        return amsg(owner, i, a_s.at[i], a_r.at[i, 1 + cls], (up, down)[d])

    def a_r_(i, cls, d, owner):
        return amsg(owner, i, a_s.at[i], a_r.at[i, 3 + cls], (up, down)[d], part=d)

    def a_d(i, owner, k):
        return amsg(owner, i, a_s.at[i], a_r.at[i, 5], twin, k=k)

    def a_got(i, k, n):
        v = xbuf.at[pl.ds(0, n * FEAT), pl.ds(0, CH)]
        rcopy(v, v, a_s.at[i], a_r.at[i, k], across).wait_recv()

    def a_ahead(i):
        a_x(i, chip).start()
        a_d(i, chip, core).start()

    def a0(i):
        a_y(i, 0, 0, chip).start()
        a_y(i, 0, 1, chip).start()

    def a1(i):
        a_got(i, 0, 1)
        a_y(i, 1, 0, xchip).start()
        a_y(i, 1, 1, xchip).start()
        a_d(i, xchip, core).start()

    def a2(i):
        for cls, base in ((0, chip), (1, xchip)):
            lo, hi = chip_of(base, 3), chip_of(base, 1)
            a_got(i, 1 + cls, 2)
            a_r_(i, cls, 0, lo).start()
            a_r_(i, cls, 1, hi).start()
            a_d(i, lo, core).start()
            a_d(i, hi, core).start()

    def a3(i):
        for cls, base in ((0, chip), (1, xchip)):
            a_got(i, 3 + cls, 1)
            a_d(i, chip_of(base, 2), core).start()

    def a4(i):
        a_got(i, 5, 8)

    for i in range(LEAD):
        a0(i)
        a_ahead(i)
    c2.wait()
    c1.wait()
    for i in range(LEAD):
        w_ahead(i)
        w0(i)

    def ss_msg(slot, k):
        return rcopy(ss.at[slot], ss.at[slot], ss_s, ss_r, (g, lax.rem(t + k, 16)))

    def ss_go(k, c):
        ss_msg(t, k).start()
        return c

    lax.fori_loop(1, 16, ss_go, 0)

    def at_rows(u):
        return pl.ds(pl.multiple_of(u * CH, CH), CH)

    def finish(a, gains, rows):
        m = jnp.mean(a * a, axis=1, keepdims=True)
        a = a * lax.rsqrt(m + EPS) * gains
        return a * cosb[rows, :] + pltpu.roll(a, HD // 2, 1) * sinb[rows, :]

    def project(rows, col):
        return lax.dot_general(
            nbuf[:, rows],
            wbuf[:, pl.ds(col, 2 * HD)],
            (((0,), (0,)), ((), ())),
            preferred_element_type=jnp.float32,
        )

    def cache_out(u):
        return pltpu.make_async_copy(cacheb.at[at_rows(u), :], cache_ref.at[at_rows(u), :], out_s.at[0])

    def unit_rows(u):
        return pl.ds(pl.multiple_of(u * UNIT, UNIT), UNIT)

    def ctx_out(u, pair):
        cols = pl.ds(pl.multiple_of(pair * 2 * HD, 2 * HD), 2 * HD)
        return pltpu.make_async_copy(ctxb.at[unit_rows(u), cols], ctx_ref.at[unit_rows(u), cols], out_s.at[1])

    def do_kv(u, c):
        inv = tinv[pl.ds(u, 1), :]

        def norm(f, c):
            rows = pl.ds(pl.multiple_of(f * 2 * FEAT, 2 * FEAT), 2 * FEAT)
            x = xbuf[rows, at_rows(u)].astype(jnp.float32)
            nbuf[rows, at_rows(u)] = (x * inv * gcol[rows, :]).astype(jnp.bfloat16)
            return c

        lax.fori_loop(0, 8, norm, 0)
        r = project(at_rows(u), 0)
        live = rows_of(u, CH, HD) < total
        key = jnp.where(live, finish(r[:, :HD], kg_ref[...], at_rows(u)), 0.0).astype(jnp.bfloat16)
        val = jnp.where(live, r[:, HD:], 0.0).astype(jnp.bfloat16)
        kbuf[at_rows(u), :] = key
        vbuf[at_rows(u), pl.ds(0, HD)] = val
        cacheb[at_rows(u), :] = jnp.where(core == 0, key, val)
        cache_out(u).start()
        return c

    def do_q(u, pair):
        r = project(unit_rows(u), pl.multiple_of(2 * HD + pair * 2 * HD, 2 * HD))
        q = [finish(r[:, h * HD:(h + 1) * HD], qg_ref[...], unit_rows(u)).astype(jnp.bfloat16) for h in range(2)]

        def attend(n):
            rows = u * UNIT + lax.broadcasted_iota(jnp.int32, (UNIT, n), 0)
            start = starts_of(u * UNIT + lax.broadcasted_iota(jnp.int32, (UNIT, HD), 0))[:, :1]
            keys = lax.broadcasted_iota(jnp.int32, (UNIT, n), 1)
            allowed = (keys >= start) & (keys <= rows)
            for h in range(2):
                s = lax.dot_general(
                    q[h], kbuf[:n, :], (((1,), (1,)), ((), ())), preferred_element_type=jnp.float32
                )
                p = jnp.where(allowed, jnp.exp2(s * (LOG2E / math.sqrt(HD))), 0.0).astype(jnp.bfloat16)
                a = jnp.dot(p, vbuf[:n, :], preferred_element_type=jnp.float32)
                cols = pl.ds(pl.multiple_of((pair * 2 + h) * HD, HD), HD)
                ctxb[unit_rows(u), cols] = (a[:, :HD] / a[:, HD:]).astype(jnp.bfloat16)

        lax.switch(u, [functools.partial(attend, UNIT * (b + 1)) for b in range(ROWS // UNIT)])
        ctx_out(u, pair).start()

    def do_task(n, c):
        unit, pair = 0, 0
        for m, (_, p, u) in enumerate(TASKS):
            unit = jnp.where(n == m, u, unit)
            pair = jnp.where(n == m, p, pair)
        do_q(unit, pair)
        return c

    def stage(k, lo, hi, fn):
        @pl.when((k >= lo) & (k < hi))
        def _():
            fn(k)

    def w_step(k):
        stage(k + LEAD, LEAD, NW, w_ahead)
        stage(k + LEAD, LEAD, NW, w0)
        stage(k, 0, NW, w1)
        stage(k - 2, 0, NW, w2)
        stage(k - 4, 0, NW, w3)
        stage(k - 4, 0, NW, w4)

    def tick(k, c):
        stage(k + LEAD, LEAD, NCH, a_ahead)
        stage(k + LEAD, LEAD, NCH, a0)
        stage(k, 0, NCH, a1)
        stage(k - 2, 0, NCH, a2)
        stage(k - 4, 0, NCH, a3)
        stage(k - 5, 0, NCH, a4)

        @pl.when(k == 0)
        def _():
            kbuf[...] = jnp.zeros_like(kbuf)
            vbuf[:, :HD] = jnp.zeros((ROWS, HD), jnp.bfloat16)
            vbuf[:, HD:] = jnp.ones((ROWS, HD), jnp.bfloat16)

        @pl.when(k == 1)
        def _():
            lax.fori_loop(0, 16 * FEAT // HD, gain_column, 0)

        @pl.when(k < NCH)
        def _():
            trig(k, 0)

        @pl.when(k == LAG)
        def _():
            v = ss.at[pl.ds(0, 15)]
            rcopy(v, v, ss_s, ss_r, twin).wait_recv()
            sums = jnp.sum(ss[...], axis=0)
            tinv[...] = lax.rsqrt(sums * (1.0 / (16 * FEAT)) + EPS)

        @pl.when(k >= LAG)
        def _():
            do_kv(k - LAG, 0)

        @pl.when(k == 0)
        def _():
            w_step(0)

        w_step(k + 1)
        before = sum(jnp.where(k > task[0], 1, 0) for task in TASKS)
        after = sum(jnp.where(k >= task[0], 1, 0) for task in TASKS)
        lax.fori_loop(before, after, do_task, 0)
        return c

    lax.fori_loop(0, NCH + LAG, tick, 0)

    v = ss.at[pl.ds(0, 15)]
    rcopy(v, v, ss_s, ss_r, twin).wait_send()

    def w_sent(i, c):
        v = wbuf.at[pl.ds(0, 7 * KH), pl.ds(0, HD)]
        rcopy(v, v, w_s.at[i], w_r.at[i, 0], twin).wait_send()

        return c

    def kv_sent(i, c):
        v = wbuf.at[pl.ds(0, 15 * KH), pl.ds(0, HD)]
        rcopy(v, v, w_s.at[i], w_r.at[i, 0], twin).wait_send()
        return c

    lax.fori_loop(0, 2, kv_sent, 0)
    lax.fori_loop(2, NW, w_sent, 0)

    def a_sent(i, c):
        v = xbuf.at[pl.ds(0, 15 * FEAT), pl.ds(0, CH)]
        rcopy(v, v, a_s.at[i], a_r.at[i, 0], twin).wait_send()
        return c

    lax.fori_loop(0, NCH, a_sent, 0)
    pltpu.make_async_copy(cacheb, cache_ref, out_s.at[0]).wait()
    pltpu.make_async_copy(ctxb, ctx_ref, out_s.at[1]).wait()


def hand_on(cache_in, ctx_in, cache_ref, ctx_ref, cache_held, ctx_held, sem):
    parts = []
    for n in range(4):
        rows = pl.ds(n * ROWS // 4, ROWS // 4)
        for a, (src, held, dst) in enumerate(((cache_in, cache_held, cache_ref), (ctx_in, ctx_held, ctx_ref))):
            parts.append(
                (
                    pltpu.make_async_copy(src.at[rows, :], held.at[rows, :], sem.at[n, a, 0]),
                    pltpu.make_async_copy(held.at[rows, :], dst.at[rows, :], sem.at[n, a, 1]),
                )
            )
    for fetch, _ in parts:
        fetch.start()
    for fetch, store in parts:
        fetch.wait()
        store.start()
    for _, store in parts:
        store.wait()


def per_device(activations, norm_gain, query_gain, key_gain, query_weight, keyval_weight, lengths):
    half = np.arange(64, dtype=np.float64)
    freq = np.exp(half * (-2.0 * math.log(THETA) / HD)).astype(np.float32)
    freq = jnp.asarray(np.concatenate([freq, freq])[None, :])
    vmem = pl.BlockSpec(memory_space=pltpu.VMEM)
    hbm = pl.BlockSpec(memory_space=pl.ANY)
    dma = pltpu.SemaphoreType.DMA
    bf16, f32 = jnp.bfloat16, jnp.float32
    cache, context = pl.pallas_call(
        kernel,
        out_shape=(
            jax.ShapeDtypeStruct((ROWS, HD), bf16),
            jax.ShapeDtypeStruct((ROWS, 4 * HD), bf16),
        ),
        in_specs=[pl.BlockSpec(memory_space=pltpu.SMEM)] + [vmem] * 5 + [hbm] * 2,
        out_specs=(hbm, hbm),
        scratch_shapes=[
            pltpu.VMEM((16 * FEAT, ROWS), bf16),
            pltpu.VMEM((16 * FEAT, ROWS), bf16),
            pltpu.VMEM((8 * WROWS, 6 * HD), bf16),
            pltpu.VMEM((16 * FEAT, HD), f32),
            pltpu.VMEM((16, 16, CH), f32),
            pltpu.VMEM((16, CH), f32),
            pltpu.VMEM((ROWS, HD), f32),
            pltpu.VMEM((ROWS, HD), f32),
            pltpu.VMEM((ROWS, HD), bf16),
            pltpu.VMEM((ROWS, 2 * HD), bf16),
            pltpu.VMEM((ROWS, HD), bf16),
            pltpu.VMEM((ROWS, 4 * HD), bf16),
            dma((2,)), dma, dma, dma((2,)),
            dma((NCH,)), dma((NCH, 6)), dma((NW,)), dma((NW, 6)),
        ],
        compiler_params=pltpu.CompilerParams(
            collective_id=0, has_side_effects=True, vmem_limit_bytes=56 * 2**20
        ),
        cost_estimate=pl.CostEstimate(
            flops=2 * ROWS * 5120 * 768, bytes_accessed=4 * 2**20, transcendentals=4 * ROWS * ROWS
        ),
    )(
        lengths,
        activations.T,
        norm_gain[None, :],
        freq,
        query_gain[None, :],
        key_gain[None, :],
        query_weight,
        keyval_weight,
    )
    return pl.pallas_call(
        hand_on,
        out_shape=(
            jax.ShapeDtypeStruct((ROWS, HD), bf16),
            jax.ShapeDtypeStruct((ROWS, 4 * HD), bf16),
        ),
        in_specs=[hbm] * 2,
        out_specs=(hbm, hbm),
        scratch_shapes=[
            pltpu.VMEM((ROWS, HD), bf16),
            pltpu.VMEM((ROWS, 4 * HD), bf16),
            dma((4, 2, 2)),
        ],
        compiler_params=pltpu.CompilerParams(vmem_limit_bytes=60 * 2**20),
    )(cache, context)


def solution(mesh):
    placed = (P("grp", "tp"), P(), P(), P(), P("grp", "tp"), P("grp", "tp"), P())
    return jax.shard_map(
        per_device,
        mesh=mesh,
        in_specs=placed,
        out_specs=(P("grp", "tp"), P("grp", "tp")),
        check_vma=False,
    )
```

```python
import functools
import math

import jax
import jax.numpy as jnp
import numpy as np
from jax import lax
from jax.experimental import pallas as pl
from jax.experimental.pallas import tpu as pltpu
from jax.sharding import PartitionSpec as P

EPS = 1e-06
THETA = 1000000.0
MESH = pl.DeviceIdType.MESH
HD = 128
ROWS = 1536
CH = 128
NCH = ROWS // CH
FEAT = 320
WROWS = 640
KH = 320
NW = 10
KTILE = 256
LAG = 5
UNIT = 2 * CH
TASKS = (
    (9, 0, 2, 0), (9, 0, 2, 1), (10, 0, 2, 2), (11, 2, 2, 0), (12, 2, 2, 1),
    (12, 2, 2, 2), (13, 0, 4, 3), (14, 0, 4, 4), (16, 0, 4, 5),
)
LEAD = 3
LOG2E = math.log2(math.e)


def kernel(
    len_ref, x_ref, gain_ref, freq_ref, qg_ref, kg_ref, wq_ref, wkv_ref,
    cache_ref, ctx_ref,
    xbuf, nbuf, wbuf, gcol, ss, tinv, startb, cosb, sinb, kbuf, vbuf, cacheb, ctxb,
    out_s, ss_s, ss_r, loc_s, a_s, a_r, w_s, w_r,
):
    g = lax.axis_index("grp")
    t = lax.axis_index("tp")
    core = lax.rem(t, 2)
    chip = t // 2
    xchip = chip + 1 - 2 * lax.rem(chip, 2)

    def chip_of(base, step):
        return lax.rem(base + 2 * step, 8)

    def tp_dev(c, k):
        return (g, c * 2 + k)

    up, down = tp_dev(chip_of(chip, 1), core), tp_dev(chip_of(chip, 3), core)
    across, twin = tp_dev(xchip, core), tp_dev(chip, 1 - core)
    gx = lax.rem(g + 4, 8)

    def ring(base, step):
        return (base // 4) * 4 + lax.rem(lax.rem(base, 4) + step, 4)

    zup, zdown, wacross = (ring(g, 1), t), (ring(g, 3), t), (gx, t)

    bar = pltpu.get_barrier_semaphore()

    def greet(k, c):
        pl.semaphore_signal(bar, inc=1, device_id=(g, lax.rem(t + k, 16)), device_id_type=MESH)
        return c

    lax.fori_loop(1, 16, greet, 0)
    for d in (zup, zdown, wacross):
        pl.semaphore_signal(bar, inc=1, device_id=d, device_id_type=MESH)

    own_w = pl.multiple_of(g * WROWS, WROWS)
    c1 = pltpu.make_async_copy(wq_ref, wbuf.at[pl.ds(own_w, WROWS), pl.ds(2 * HD, 4 * HD)], loc_s.at[0])
    c2 = pltpu.make_async_copy(
        wkv_ref, wbuf.at[pl.ds(own_w, WROWS), pl.ds(pl.multiple_of(core * HD, HD), HD)], loc_s.at[1]
    )
    c1.start()
    c2.start()
    own_f = pl.multiple_of(t * FEAT, FEAT)
    ss[t] = jnp.zeros((16, CH), jnp.float32)

    def stage_own(i, c):
        cols = pl.ds(pl.multiple_of(i * CH, CH), CH)
        mine = x_ref[:, cols]
        xbuf[pl.ds(own_f, FEAT), cols] = mine
        mine = mine.astype(jnp.float32)
        ss[t, pl.ds(i, 1), :] = jnp.sum(mine * mine, axis=0, keepdims=True)
        return c

    lax.fori_loop(0, NCH, stage_own, 0)


    ends = []
    total = 0
    for r in range(8):
        total = total + len_ref[g, r]
        ends.append(total)

    def starts_of(rows):
        start = jnp.zeros_like(rows)
        for r in range(8):
            start = start + jnp.where(rows >= ends[r], len_ref[g, r], 0)
        return start

    def rows_of(u, n, lanes):
        return u * CH + lax.broadcasted_iota(jnp.int32, (n, lanes), 0)

    def trig(u, c):
        rows = rows_of(u, CH, HD)
        start = starts_of(rows)
        angle = (rows - start).astype(jnp.float32) * freq_ref[...]
        lane = lax.broadcasted_iota(jnp.int32, (CH, HD), 1)
        at = pl.ds(pl.multiple_of(u * CH, CH), CH)
        startb[at, :] = start
        cosb[at, :] = jnp.cos(angle)
        sinb[at, :] = jnp.where(lane < HD // 2, -1.0, 1.0) * jnp.sin(angle)
        return c


    def gain_column(f, c):
        at = pl.ds(pl.multiple_of(f * HD, HD), HD)
        gcol[at, :] = jnp.transpose(jnp.broadcast_to(gain_ref[:, at], (HD, HD)))
        return c

    pl.semaphore_wait(bar, 18)

    def rcopy(src, dst, s, r, dev):
        return pltpu.make_async_remote_copy(
            src_ref=src, dst_ref=dst, send_sem=s, recv_sem=r, device_id=dev, device_id_type=MESH
        )

    def wview(owner, i, part=None):
        j = i // 2
        col = pl.multiple_of(jnp.where(j == 0, core * HD, HD + HD * j), HD)
        row = owner * WROWS + lax.rem(i, 2) * KH
        n = KH
        if part is not None:
            n = KH // 2
            row = row + part * n
        return wbuf.at[pl.ds(pl.multiple_of(row, 32), n), pl.ds(col, HD)]

    def wmsg(owner, i, s, r, dev, part=None):
        v = wview(owner, i, part)
        return rcopy(v, v, s, r, dev)

    def w_x(i, owner):
        return wmsg(owner, i, w_s.at[i], w_r.at[i, 0], wacross)

    def w_z(i, cls, d, owner):
        return wmsg(owner, i, w_s.at[i], w_r.at[i, 1 + cls], (zup, zdown)[d])

    def w_r_(i, cls, d, owner):
        return wmsg(owner, i, w_s.at[i], w_r.at[i, 3 + cls], (zup, zdown)[d], part=d)

    def w_got(i, k, n):
        v = wbuf.at[pl.ds(0, n * KH), pl.ds(0, HD)]
        rcopy(v, v, w_s.at[i], w_r.at[i, k], wacross).wait_recv()

    def kvview(i, slot, col):
        row = slot * WROWS + i * KH
        return wbuf.at[pl.ds(pl.multiple_of(row, 32), KH), pl.ds(pl.multiple_of(col * HD, HD), HD)]

    def w_d(i, owner, col):
        v = kvview(i, owner, col)
        return rcopy(v, v, w_s.at[i], w_r.at[i, 5], twin)

    def w_share(i, owner):
        @pl.when(i < 2)
        def _():
            w_d(i, owner, core).start()

    def w_ahead(i):
        w_x(i, g).start()
        w_share(i, g)

    def w0(i):
        w_z(i, 0, 0, g).start()
        w_z(i, 0, 1, g).start()

    def mixed(i):
        return i < 0

    def w_f(i, n, owner):
        return wmsg(owner, i, w_s.at[i], w_r.at[i, (2, 2, 4)[n]], wacross)

    def w1(i):
        w_got(i, 0, 1)

        @pl.when(jnp.logical_not(mixed(i)))
        def _():
            w_z(i, 1, 0, gx).start()
            w_z(i, 1, 1, gx).start()

        w_share(i, gx)

    def w2(i):
        def near(cls, base):
            lo, hi = ring(base, 3), ring(base, 1)
            w_got(i, 1 + cls, 2)
            w_r_(i, cls, 0, lo).start()
            w_r_(i, cls, 1, hi).start()
            w_share(i, lo)
            w_share(i, hi)

        near(0, g)

        @pl.when(mixed(i))
        def _():
            w_f(i, 0, ring(g, 3)).start()
            w_f(i, 1, ring(g, 1)).start()

        @pl.when(jnp.logical_not(mixed(i)))
        def _():
            near(1, gx)

    def w3(i):
        w_got(i, 3, 1)
        w_share(i, ring(g, 2))

        @pl.when(mixed(i))
        def _():
            w_f(i, 2, ring(g, 2)).start()

        @pl.when(jnp.logical_not(mixed(i)))
        def _():
            w_got(i, 4, 1)
            w_share(i, ring(gx, 2))

    def w4(i):
        @pl.when(i < 2)
        def _():
            w_got(i, 5, 8)

        @pl.when(mixed(i))
        def _():
            w_got(i, 2, 2)
            w_got(i, 4, 1)

    def aview(owner, i, k, part=None):
        row = (owner * 2 + k) * FEAT
        n = FEAT
        if part is not None:
            n = FEAT // 2
            row = row + part * n
        return xbuf.at[pl.ds(pl.multiple_of(row, 32), n), pl.ds(pl.multiple_of(i * CH, CH), CH)]

    def amsg(owner, i, s, r, dev, part=None, k=None):
        v = aview(owner, i, core if k is None else k, part)
        return rcopy(v, v, s, r, dev)

    def a_x(i, owner):
        return amsg(owner, i, a_s.at[i], a_r.at[i, 0], across)

    def a_y(i, cls, d, owner):
        return amsg(owner, i, a_s.at[i], a_r.at[i, 1 + cls], (up, down)[d])

    def a_r_(i, cls, d, owner):
        return amsg(owner, i, a_s.at[i], a_r.at[i, 3 + cls], (up, down)[d], part=d)

    def a_d(i, owner, k):
        return amsg(owner, i, a_s.at[i], a_r.at[i, 5], twin, k=k)

    def a_got(i, k, n):
        v = xbuf.at[pl.ds(0, n * FEAT), pl.ds(0, CH)]
        rcopy(v, v, a_s.at[i], a_r.at[i, k], across).wait_recv()

    def a_ahead(i):
        a_x(i, chip).start()
        a_d(i, chip, core).start()

    def a0(i):
        a_y(i, 0, 0, chip).start()
        a_y(i, 0, 1, chip).start()

    def a1(i):
        a_got(i, 0, 1)
        a_y(i, 1, 0, xchip).start()
        a_y(i, 1, 1, xchip).start()
        a_d(i, xchip, core).start()

    def a2(i):
        for cls, base in ((0, chip), (1, xchip)):
            lo, hi = chip_of(base, 3), chip_of(base, 1)
            a_got(i, 1 + cls, 2)
            a_r_(i, cls, 0, lo).start()
            a_r_(i, cls, 1, hi).start()
            a_d(i, lo, core).start()
            a_d(i, hi, core).start()

    def a3(i):
        for cls, base in ((0, chip), (1, xchip)):
            a_got(i, 3 + cls, 1)
            a_d(i, chip_of(base, 2), core).start()

    def a4(i):
        a_got(i, 5, 8)

    for i in range(LEAD):
        a0(i)
        a_ahead(i)
    c2.wait()
    c1.wait()
    for i in range(LEAD):
        w_ahead(i)
        w0(i)

    def ss_msg(slot, k):
        return rcopy(ss.at[slot], ss.at[slot], ss_s, ss_r, (g, lax.rem(t + k, 16)))

    def ss_go(k, c):
        ss_msg(t, k).start()
        return c

    lax.fori_loop(1, 16, ss_go, 0)

    def at_rows(u):
        return pl.ds(pl.multiple_of(u * CH, CH), CH)

    def finish(a, gains, rows):
        m = jnp.mean(a * a, axis=1, keepdims=True)
        a = a * lax.rsqrt(m + EPS) * gains
        return a * cosb[rows, :] + pltpu.roll(a, HD // 2, 1) * sinb[rows, :]

    def project(rows, col, n):
        return lax.dot_general(
            nbuf[:, rows],
            wbuf[:, pl.ds(col, n)],
            (((0,), (0,)), ((), ())),
            preferred_element_type=jnp.float32,
        )

    def cache_out(u):
        return pltpu.make_async_copy(cacheb.at[at_rows(u), :], cache_ref.at[at_rows(u), :], out_s.at[0])

    def unit_rows(u):
        return pl.ds(pl.multiple_of(u * UNIT, UNIT), UNIT)

    def ctx_out(u, first, heads):
        cols = pl.ds(pl.multiple_of(first * HD, HD), heads * HD)
        return pltpu.make_async_copy(ctxb.at[unit_rows(u), cols], ctx_ref.at[unit_rows(u), cols], out_s.at[1])

    def do_kv(u, c):
        inv = tinv[pl.ds(u, 1), :]

        def norm(f, c):
            rows = pl.ds(pl.multiple_of(f * 2 * FEAT, 2 * FEAT), 2 * FEAT)
            x = xbuf[rows, at_rows(u)].astype(jnp.float32)
            nbuf[rows, at_rows(u)] = (x * inv * gcol[rows, :]).astype(jnp.bfloat16)
            return c

        lax.fori_loop(0, 8, norm, 0)
        r = project(at_rows(u), 0, 2 * HD)
        live = rows_of(u, CH, HD) < total
        key = jnp.where(live, finish(r[:, :HD], kg_ref[...], at_rows(u)), 0.0).astype(jnp.bfloat16)
        val = jnp.where(live, r[:, HD:], 0.0).astype(jnp.bfloat16)
        kbuf[at_rows(u), :] = key
        vbuf[at_rows(u), pl.ds(0, HD)] = val
        cacheb[at_rows(u), :] = jnp.where(core == 0, key, val)
        cache_out(u).start()
        return c

    def do_q(heads, units, u, first):
        r = project(unit_rows(u), pl.multiple_of((2 + first) * HD, HD), heads * HD)
        q = [
            finish(r[:, h * HD:(h + 1) * HD], qg_ref[...], unit_rows(u)).astype(jnp.bfloat16)
            for h in range(heads)
        ]

        def attend(n):
            rows = u * UNIT + lax.broadcasted_iota(jnp.int32, (UNIT, n), 0)
            start = startb[unit_rows(u), :1]
            keys = lax.broadcasted_iota(jnp.int32, (UNIT, n), 1)
            allowed = (keys >= start) & (keys <= rows)
            for h in range(heads):
                s = lax.dot_general(
                    q[h], kbuf[:n, :], (((1,), (1,)), ((), ())), preferred_element_type=jnp.float32
                )
                p = jnp.where(allowed, jnp.exp2(s * (LOG2E / math.sqrt(HD))), 0.0).astype(jnp.bfloat16)
                a = jnp.dot(p, vbuf[:n, :], preferred_element_type=jnp.float32)
                cols = pl.ds(pl.multiple_of((first + h) * HD, HD), HD)
                ctxb[unit_rows(u), cols] = (a[:, :HD] / a[:, HD:]).astype(jnp.bfloat16)

        lax.switch(u - units[0], [functools.partial(attend, UNIT * (b + 1)) for b in units])
        ctx_out(u, first, heads).start()

    def do_task(n, c):
        unit, first, heads = 0, 0, 0
        for m, (_, f, h, u) in enumerate(TASKS):
            unit = jnp.where(n == m, u, unit)
            first = jnp.where(n == m, f, first)
            heads = jnp.where(n == m, h // 4, heads)
        lax.switch(
            heads,
            [functools.partial(do_q, h, us) for h, us in ((2, range(4)), (4, range(2, 6)))],
            unit,
            first,
        )
        return c

    def stage(k, lo, hi, fn):
        @pl.when((k >= lo) & (k < hi))
        def _():
            fn(k)

    def w_step(k):
        stage(k + LEAD, LEAD, NW, w_ahead)
        stage(k + LEAD, LEAD, NW, w0)
        stage(k, 0, NW, w1)
        stage(k - 2, 0, NW - 1, w2)
        stage(k - 1, NW - 1, NW, w2)
        stage(k - 4, 0, NW - 2, w3)
        stage(k - 3, NW - 2, NW - 1, w3)
        stage(k - 2, NW - 1, NW, w3)
        stage(k - 4, 0, NW, w4)

    def tick(k, c):
        stage(k + LEAD, LEAD, NCH, a_ahead)
        stage(k + LEAD, LEAD, NCH, a0)
        stage(k, 0, NCH, a1)
        stage(k - 2, 0, NCH, a2)
        stage(k - 4, 0, NCH, a3)
        stage(k - 5, 0, NCH, a4)

        @pl.when(k == 0)
        def _():
            kbuf[...] = jnp.zeros_like(kbuf)
            vbuf[:, :HD] = jnp.zeros((ROWS, HD), jnp.bfloat16)
            vbuf[:, HD:] = jnp.ones((ROWS, HD), jnp.bfloat16)

        @pl.when(k == 1)
        def _():
            lax.fori_loop(0, 16 * FEAT // HD, gain_column, 0)

        @pl.when(k < NCH // 2)
        def _():
            lax.fori_loop(2 * k, 2 * k + 2, trig, 0)

        @pl.when(k == LAG)
        def _():
            v = ss.at[pl.ds(0, 15)]
            rcopy(v, v, ss_s, ss_r, twin).wait_recv()
            sums = jnp.sum(ss[...], axis=0)
            tinv[...] = lax.rsqrt(sums * (1.0 / (16 * FEAT)) + EPS)

        w_step(k)

        @pl.when(k >= LAG)
        def _():
            do_kv(k - LAG, 0)

        before = sum(jnp.where(k > task[0], 1, 0) for task in TASKS)
        after = sum(jnp.where(k >= task[0], 1, 0) for task in TASKS)
        lax.fori_loop(before, after, do_task, 0)
        return c

    lax.fori_loop(0, NCH + LAG, tick, 0)

    v = ss.at[pl.ds(0, 15)]
    rcopy(v, v, ss_s, ss_r, twin).wait_send()

    def w_sent(i, c):
        v = wbuf.at[pl.ds(0, 7 * KH), pl.ds(0, HD)]
        rcopy(v, v, w_s.at[i], w_r.at[i, 0], twin).wait_send()

        return c

    def kv_sent(i, c):
        v = wbuf.at[pl.ds(0, 15 * KH), pl.ds(0, HD)]
        rcopy(v, v, w_s.at[i], w_r.at[i, 0], twin).wait_send()
        return c

    lax.fori_loop(0, 2, kv_sent, 0)
    lax.fori_loop(2, NW, w_sent, 0)

    def a_sent(i, c):
        v = xbuf.at[pl.ds(0, 15 * FEAT), pl.ds(0, CH)]
        rcopy(v, v, a_s.at[i], a_r.at[i, 0], twin).wait_send()
        return c

    lax.fori_loop(0, NCH, a_sent, 0)
    pltpu.make_async_copy(cacheb, cache_ref, out_s.at[0]).wait()
    pltpu.make_async_copy(ctxb, ctx_ref, out_s.at[1]).wait()


def hand_on(cache_in, ctx_in, cache_ref, ctx_ref, cache_held, ctx_held, sem):
    parts = []
    for n in range(4):
        rows = pl.ds(n * ROWS // 4, ROWS // 4)
        for a, (src, held, dst) in enumerate(((cache_in, cache_held, cache_ref), (ctx_in, ctx_held, ctx_ref))):
            parts.append(
                (
                    pltpu.make_async_copy(src.at[rows, :], held.at[rows, :], sem.at[n, a, 0]),
                    pltpu.make_async_copy(held.at[rows, :], dst.at[rows, :], sem.at[n, a, 1]),
                )
            )
    for fetch, _ in parts:
        fetch.start()
    for fetch, store in parts:
        fetch.wait()
        store.start()
    for _, store in parts:
        store.wait()


def per_device(activations, norm_gain, query_gain, key_gain, query_weight, keyval_weight, lengths):
    half = np.arange(64, dtype=np.float64)
    freq = np.exp(half * (-2.0 * math.log(THETA) / HD)).astype(np.float32)
    freq = jnp.asarray(np.concatenate([freq, freq])[None, :])
    vmem = pl.BlockSpec(memory_space=pltpu.VMEM)
    hbm = pl.BlockSpec(memory_space=pl.ANY)
    dma = pltpu.SemaphoreType.DMA
    bf16, f32 = jnp.bfloat16, jnp.float32
    cache, context = pl.pallas_call(
        kernel,
        out_shape=(
            jax.ShapeDtypeStruct((ROWS, HD), bf16),
            jax.ShapeDtypeStruct((ROWS, 4 * HD), bf16),
        ),
        in_specs=[pl.BlockSpec(memory_space=pltpu.SMEM)] + [vmem] * 5 + [hbm] * 2,
        out_specs=(hbm, hbm),
        scratch_shapes=[
            pltpu.VMEM((16 * FEAT, ROWS), bf16),
            pltpu.VMEM((16 * FEAT, ROWS), bf16),
            pltpu.VMEM((8 * WROWS, 6 * HD), bf16),
            pltpu.VMEM((16 * FEAT, HD), f32),
            pltpu.VMEM((16, 16, CH), f32),
            pltpu.VMEM((16, CH), f32),
            pltpu.VMEM((ROWS, HD), jnp.int32),
            pltpu.VMEM((ROWS, HD), f32),
            pltpu.VMEM((ROWS, HD), f32),
            pltpu.VMEM((ROWS, HD), bf16),
            pltpu.VMEM((ROWS, 2 * HD), bf16),
            pltpu.VMEM((ROWS, HD), bf16),
            pltpu.VMEM((ROWS, 4 * HD), bf16),
            dma((2,)), dma, dma, dma((2,)),
            dma((NCH,)), dma((NCH, 6)), dma((NW,)), dma((NW, 6)),
        ],
        compiler_params=pltpu.CompilerParams(
            collective_id=0, has_side_effects=True, vmem_limit_bytes=56 * 2**20
        ),
        cost_estimate=pl.CostEstimate(
            flops=2 * ROWS * 5120 * 768, bytes_accessed=4 * 2**20, transcendentals=4 * ROWS * ROWS
        ),
    )(
        lengths,
        activations.T,
        norm_gain[None, :],
        freq,
        query_gain[None, :],
        key_gain[None, :],
        query_weight,
        keyval_weight,
    )
    return pl.pallas_call(
        hand_on,
        out_shape=(
            jax.ShapeDtypeStruct((ROWS, HD), bf16),
            jax.ShapeDtypeStruct((ROWS, 4 * HD), bf16),
        ),
        in_specs=[hbm] * 2,
        out_specs=(hbm, hbm),
        scratch_shapes=[
            pltpu.VMEM((ROWS, HD), bf16),
            pltpu.VMEM((ROWS, 4 * HD), bf16),
            dma((4, 2, 2)),
        ],
        compiler_params=pltpu.CompilerParams(vmem_limit_bytes=60 * 2**20),
    )(cache, context)


def solution(mesh):
    placed = (P("grp", "tp"), P(), P(), P(), P("grp", "tp"), P("grp", "tp"), P())
    return jax.shard_map(
        per_device,
        mesh=mesh,
        in_specs=placed,
        out_specs=(P("grp", "tp"), P("grp", "tp")),
        check_vma=False,
    )
```

```python
import functools
import math

import jax
import jax.numpy as jnp
import numpy as np
from jax import lax
from jax.experimental import pallas as pl
from jax.experimental.pallas import tpu as pltpu
from jax.sharding import PartitionSpec as P

EPS = 1e-06
THETA = 1000000.0
MESH = pl.DeviceIdType.MESH
HD = 128
ROWS = 1536
CH = 128
NCH = ROWS // CH
FEAT = 320
WROWS = 640
KH = 320
NW = 10
KTILE = 256
LAG = 5
UNIT = 2 * CH
TASKS = (
    (9, 0, 2, 0), (9, 0, 2, 1), (10, 0, 2, 2), (11, 2, 2, 0), (12, 2, 2, 1),
    (12, 2, 2, 2), (13, 0, 4, 3), (14, 0, 4, 4), (16, 0, 4, 5),
)
LEAD = 3
LOG2E = math.log2(math.e)


def kernel(
    len_ref, x_ref, gain_ref, freq_ref, qg_ref, kg_ref, wq_ref, wkv_ref,
    cache_ref, ctx_ref,
    xbuf, nbuf, wbuf, gcol, ss, tinv, startb, cosb, sinb, kbuf, vbuf, cacheb, ctxb,
    out_s, ss_s, ss_r, loc_s, a_s, a_r, w_s, w_r,
):
    g = lax.axis_index("grp")
    t = lax.axis_index("tp")
    core = lax.rem(t, 2)
    chip = t // 2
    xchip = chip + 1 - 2 * lax.rem(chip, 2)

    def chip_of(base, step):
        return lax.rem(base + 2 * step, 8)

    def tp_dev(c, k):
        return (g, c * 2 + k)

    up, down = tp_dev(chip_of(chip, 1), core), tp_dev(chip_of(chip, 3), core)
    across, twin = tp_dev(xchip, core), tp_dev(chip, 1 - core)
    gx = lax.rem(g + 4, 8)

    def ring(base, step):
        return (base // 4) * 4 + lax.rem(lax.rem(base, 4) + step, 4)

    zup, zdown, wacross = (ring(g, 1), t), (ring(g, 3), t), (gx, t)

    bar = pltpu.get_barrier_semaphore()

    def greet(k, c):
        pl.semaphore_signal(bar, inc=1, device_id=(g, lax.rem(t + k, 16)), device_id_type=MESH)
        return c

    lax.fori_loop(1, 16, greet, 0)
    for d in (zup, zdown, wacross):
        pl.semaphore_signal(bar, inc=1, device_id=d, device_id_type=MESH)

    own_w = pl.multiple_of(g * WROWS, WROWS)
    c1 = pltpu.make_async_copy(wq_ref, wbuf.at[pl.ds(own_w, WROWS), pl.ds(2 * HD, 4 * HD)], loc_s.at[0])
    c2 = pltpu.make_async_copy(
        wkv_ref, wbuf.at[pl.ds(own_w, WROWS), pl.ds(pl.multiple_of(core * HD, HD), HD)], loc_s.at[1]
    )
    c1.start()
    c2.start()
    own_f = pl.multiple_of(t * FEAT, FEAT)
    ss[t] = jnp.zeros((16, CH), jnp.float32)

    def stage_own(i, c):
        cols = pl.ds(pl.multiple_of(i * CH, CH), CH)
        mine = x_ref[:, cols]
        xbuf[pl.ds(own_f, FEAT), cols] = mine
        mine = mine.astype(jnp.float32)
        ss[t, pl.ds(i, 1), :] = jnp.sum(mine * mine, axis=0, keepdims=True)
        return c

    lax.fori_loop(0, NCH, stage_own, 0)


    ends = []
    total = 0
    for r in range(8):
        total = total + len_ref[g, r]
        ends.append(total)

    def starts_of(rows):
        start = jnp.zeros_like(rows)
        for r in range(8):
            start = start + jnp.where(rows >= ends[r], len_ref[g, r], 0)
        return start

    def rows_of(u, n, lanes):
        return u * CH + lax.broadcasted_iota(jnp.int32, (n, lanes), 0)

    def trig(u, c):
        rows = rows_of(u, CH, HD)
        start = starts_of(rows)
        angle = (rows - start).astype(jnp.float32) * freq_ref[...]
        lane = lax.broadcasted_iota(jnp.int32, (CH, HD), 1)
        at = pl.ds(pl.multiple_of(u * CH, CH), CH)
        startb[at, :] = start
        cosb[at, :] = jnp.cos(angle)
        sinb[at, :] = jnp.where(lane < HD // 2, -1.0, 1.0) * jnp.sin(angle)
        return c


    def gain_column(f, c):
        at = pl.ds(pl.multiple_of(f * HD, HD), HD)
        gcol[at, :] = jnp.transpose(jnp.broadcast_to(gain_ref[:, at], (HD, HD)))
        return c

    pl.semaphore_wait(bar, 18)

    def rcopy(src, dst, s, r, dev):
        return pltpu.make_async_remote_copy(
            src_ref=src, dst_ref=dst, send_sem=s, recv_sem=r, device_id=dev, device_id_type=MESH
        )

    def wview(owner, i, part=None):
        j = i // 2
        col = pl.multiple_of(jnp.where(j == 0, core * HD, HD + HD * j), HD)
        row = owner * WROWS + lax.rem(i, 2) * KH
        n = KH
        if part is not None:
            n = KH // 2
            row = row + part * n
        return wbuf.at[pl.ds(pl.multiple_of(row, 32), n), pl.ds(col, HD)]

    def wmsg(owner, i, s, r, dev, part=None):
        v = wview(owner, i, part)
        return rcopy(v, v, s, r, dev)

    def w_x(i, owner):
        return wmsg(owner, i, w_s.at[i], w_r.at[i, 0], wacross)

    def w_z(i, cls, d, owner):
        return wmsg(owner, i, w_s.at[i], w_r.at[i, 1 + cls], (zup, zdown)[d])

    def w_r_(i, cls, d, owner):
        return wmsg(owner, i, w_s.at[i], w_r.at[i, 3 + cls], (zup, zdown)[d], part=d)

    def w_got(i, k, n):
        v = wbuf.at[pl.ds(0, n * KH), pl.ds(0, HD)]
        rcopy(v, v, w_s.at[i], w_r.at[i, k], wacross).wait_recv()

    def kvview(i, slot, col):
        row = slot * WROWS + i * KH
        return wbuf.at[pl.ds(pl.multiple_of(row, 32), KH), pl.ds(pl.multiple_of(col * HD, HD), HD)]

    def w_d(i, owner, col):
        v = kvview(i, owner, col)
        return rcopy(v, v, w_s.at[i], w_r.at[i, 5], twin)

    def w_share(i, owner):
        @pl.when(i < 2)
        def _():
            w_d(i, owner, core).start()

    def w_ahead(i):
        w_x(i, g).start()
        w_share(i, g)

    def w0(i):
        w_z(i, 0, 0, g).start()
        w_z(i, 0, 1, g).start()

    def mixed(i):
        return i < 0

    def w_f(i, n, owner):
        return wmsg(owner, i, w_s.at[i], w_r.at[i, (2, 2, 4)[n]], wacross)

    def w1(i):
        w_got(i, 0, 1)

        @pl.when(jnp.logical_not(mixed(i)))
        def _():
            w_z(i, 1, 0, gx).start()
            w_z(i, 1, 1, gx).start()

        w_share(i, gx)

    def w2(i):
        def near(cls, base):
            lo, hi = ring(base, 3), ring(base, 1)
            w_got(i, 1 + cls, 2)
            w_r_(i, cls, 0, lo).start()
            w_r_(i, cls, 1, hi).start()
            w_share(i, lo)
            w_share(i, hi)

        near(0, g)

        @pl.when(mixed(i))
        def _():
            w_f(i, 0, ring(g, 3)).start()
            w_f(i, 1, ring(g, 1)).start()

        @pl.when(jnp.logical_not(mixed(i)))
        def _():
            near(1, gx)

    def w3(i):
        w_got(i, 3, 1)
        w_share(i, ring(g, 2))

        @pl.when(mixed(i))
        def _():
            w_f(i, 2, ring(g, 2)).start()

        @pl.when(jnp.logical_not(mixed(i)))
        def _():
            w_got(i, 4, 1)
            w_share(i, ring(gx, 2))

    def w4(i):
        @pl.when(i < 2)
        def _():
            w_got(i, 5, 8)

        @pl.when(mixed(i))
        def _():
            w_got(i, 2, 2)
            w_got(i, 4, 1)

    def aview(owner, i, k, part=None):
        row = (owner * 2 + k) * FEAT
        n = FEAT
        if part is not None:
            n = FEAT // 2
            row = row + part * n
        return xbuf.at[pl.ds(pl.multiple_of(row, 32), n), pl.ds(pl.multiple_of(i * CH, CH), CH)]

    def amsg(owner, i, s, r, dev, part=None, k=None):
        v = aview(owner, i, core if k is None else k, part)
        return rcopy(v, v, s, r, dev)

    def a_x(i, owner):
        return amsg(owner, i, a_s.at[i], a_r.at[i, 0], across)

    def a_y(i, cls, d, owner):
        return amsg(owner, i, a_s.at[i], a_r.at[i, 1 + cls], (up, down)[d])

    def a_r_(i, cls, d, owner):
        return amsg(owner, i, a_s.at[i], a_r.at[i, 3 + cls], (up, down)[d], part=d)

    def a_d(i, owner, k):
        return amsg(owner, i, a_s.at[i], a_r.at[i, 5], twin, k=k)

    def a_got(i, k, n):
        v = xbuf.at[pl.ds(0, n * FEAT), pl.ds(0, CH)]
        rcopy(v, v, a_s.at[i], a_r.at[i, k], across).wait_recv()

    def a_ahead(i):
        a_x(i, chip).start()
        a_d(i, chip, core).start()

    def a0(i):
        a_y(i, 0, 0, chip).start()
        a_y(i, 0, 1, chip).start()

    def a1(i):
        a_got(i, 0, 1)
        a_y(i, 1, 0, xchip).start()
        a_y(i, 1, 1, xchip).start()
        a_d(i, xchip, core).start()

    def a2(i):
        for cls, base in ((0, chip), (1, xchip)):
            lo, hi = chip_of(base, 3), chip_of(base, 1)
            a_got(i, 1 + cls, 2)
            a_r_(i, cls, 0, lo).start()
            a_r_(i, cls, 1, hi).start()
            a_d(i, lo, core).start()
            a_d(i, hi, core).start()

    def a3(i):
        for cls, base in ((0, chip), (1, xchip)):
            a_got(i, 3 + cls, 1)
            a_d(i, chip_of(base, 2), core).start()

    def a4(i):
        a_got(i, 5, 8)

    for i in range(LEAD):
        a0(i)
        a_ahead(i)
    c2.wait()
    c1.wait()
    for i in range(LEAD):
        w_ahead(i)
        w0(i)

    def ss_msg(slot, k):
        return rcopy(ss.at[slot], ss.at[slot], ss_s, ss_r, (g, lax.rem(t + k, 16)))

    def ss_go(k, c):
        ss_msg(t, k).start()
        return c

    lax.fori_loop(1, 16, ss_go, 0)

    def at_rows(u):
        return pl.ds(pl.multiple_of(u * CH, CH), CH)

    def finish(a, gains, rows):
        m = jnp.mean(a * a, axis=1, keepdims=True)
        a = a * lax.rsqrt(m + EPS) * gains
        return a * cosb[rows, :] + pltpu.roll(a, HD // 2, 1) * sinb[rows, :]

    def project(rows, col, n):
        return lax.dot_general(
            nbuf[:, rows],
            wbuf[:, pl.ds(col, n)],
            (((0,), (0,)), ((), ())),
            preferred_element_type=jnp.float32,
        )

    def cache_out(u):
        return pltpu.make_async_copy(cacheb.at[unit_rows(u), :], cache_ref.at[unit_rows(u), :], out_s.at[0])

    def unit_rows(u):
        return pl.ds(pl.multiple_of(u * UNIT, UNIT), UNIT)

    def ctx_out(u, first, heads):
        cols = pl.ds(pl.multiple_of(first * HD, HD), heads * HD)
        return pltpu.make_async_copy(ctxb.at[unit_rows(u), cols], ctx_ref.at[unit_rows(u), cols], out_s.at[1])

    def do_kv(u, c):
        inv = tinv[pl.ds(u, 1), :]

        def norm(f, c):
            rows = pl.ds(pl.multiple_of(f * 2 * FEAT, 2 * FEAT), 2 * FEAT)
            x = xbuf[rows, at_rows(u)].astype(jnp.float32)
            nbuf[rows, at_rows(u)] = (x * inv * gcol[rows, :]).astype(jnp.bfloat16)
            return c

        lax.fori_loop(0, 8, norm, 0)

        @pl.when(lax.rem(u, 2) == 1)
        def _():
            n = u // 2
            rows = unit_rows(n)
            r = project(rows, 0, 2 * HD)
            live = n * UNIT + lax.broadcasted_iota(jnp.int32, (UNIT, HD), 0) < total
            key = jnp.where(live, finish(r[:, :HD], kg_ref[...], rows), 0.0).astype(jnp.bfloat16)
            val = jnp.where(live, r[:, HD:], 0.0).astype(jnp.bfloat16)
            kbuf[rows, :] = key
            vbuf[rows, pl.ds(0, HD)] = val
            cacheb[rows, :] = jnp.where(core == 0, key, val)
            cache_out(n).start()

        return c

    def do_q(heads, units, u, first):
        r = project(unit_rows(u), pl.multiple_of((2 + first) * HD, HD), heads * HD)
        q = [
            finish(r[:, h * HD:(h + 1) * HD], qg_ref[...], unit_rows(u)).astype(jnp.bfloat16)
            for h in range(heads)
        ]

        def attend(n):
            rows = u * UNIT + lax.broadcasted_iota(jnp.int32, (UNIT, n), 0)
            start = startb[unit_rows(u), :1]
            keys = lax.broadcasted_iota(jnp.int32, (UNIT, n), 1)
            allowed = (keys >= start) & (keys <= rows)
            for h in range(heads):
                s = lax.dot_general(
                    q[h], kbuf[:n, :], (((1,), (1,)), ((), ())), preferred_element_type=jnp.float32
                )
                p = jnp.where(allowed, jnp.exp2(s * (LOG2E / math.sqrt(HD))), 0.0).astype(jnp.bfloat16)
                a = jnp.dot(p, vbuf[:n, :], preferred_element_type=jnp.float32)
                cols = pl.ds(pl.multiple_of((first + h) * HD, HD), HD)
                ctxb[unit_rows(u), cols] = (a[:, :HD] / a[:, HD:]).astype(jnp.bfloat16)

        lax.switch(u - units[0], [functools.partial(attend, UNIT * (b + 1)) for b in units])
        ctx_out(u, first, heads).start()

    def do_task(n, c):
        unit, first, heads = 0, 0, 0
        for m, (_, f, h, u) in enumerate(TASKS):
            unit = jnp.where(n == m, u, unit)
            first = jnp.where(n == m, f, first)
            heads = jnp.where(n == m, h // 4, heads)
        lax.switch(
            heads,
            [functools.partial(do_q, h, us) for h, us in ((2, range(4)), (4, range(2, 6)))],
            unit,
            first,
        )
        return c

    def stage(k, lo, hi, fn):
        @pl.when((k >= lo) & (k < hi))
        def _():
            fn(k)

    def w_step(k):
        stage(k + LEAD, LEAD, NW, w_ahead)
        stage(k + LEAD, LEAD, NW, w0)
        stage(k, 0, NW, w1)
        stage(k - 2, 0, NW - 1, w2)
        stage(k - 1, NW - 1, NW, w2)
        stage(k - 4, 0, NW - 2, w3)
        stage(k - 3, NW - 2, NW - 1, w3)
        stage(k - 2, NW - 1, NW, w3)
        stage(k - 4, 0, NW, w4)

    def tick(k, c):
        stage(k + LEAD, LEAD, NCH, a_ahead)
        stage(k + LEAD, LEAD, NCH, a0)
        stage(k, 0, NCH, a1)
        stage(k - 2, 0, NCH, a2)
        stage(k - 4, 0, NCH, a3)
        stage(k - 5, 0, NCH, a4)

        @pl.when(k == 0)
        def _():
            kbuf[...] = jnp.zeros_like(kbuf)
            vbuf[:, :HD] = jnp.zeros((ROWS, HD), jnp.bfloat16)
            vbuf[:, HD:] = jnp.ones((ROWS, HD), jnp.bfloat16)

        @pl.when(k == 1)
        def _():
            lax.fori_loop(0, 16 * FEAT // HD, gain_column, 0)

        @pl.when(k < NCH // 2)
        def _():
            lax.fori_loop(2 * k, 2 * k + 2, trig, 0)

        @pl.when(k == LAG)
        def _():
            v = ss.at[pl.ds(0, 15)]
            rcopy(v, v, ss_s, ss_r, twin).wait_recv()
            sums = jnp.sum(ss[...], axis=0)
            tinv[...] = lax.rsqrt(sums * (1.0 / (16 * FEAT)) + EPS)

        w_step(k)

        @pl.when(k >= LAG)
        def _():
            do_kv(k - LAG, 0)

        before = sum(jnp.where(k > task[0], 1, 0) for task in TASKS)
        after = sum(jnp.where(k >= task[0], 1, 0) for task in TASKS)
        lax.fori_loop(before, after, do_task, 0)
        return c

    lax.fori_loop(0, NCH + LAG, tick, 0)

    v = ss.at[pl.ds(0, 15)]
    rcopy(v, v, ss_s, ss_r, twin).wait_send()

    def w_sent(i, c):
        v = wbuf.at[pl.ds(0, 7 * KH), pl.ds(0, HD)]
        rcopy(v, v, w_s.at[i], w_r.at[i, 0], twin).wait_send()

        return c

    def kv_sent(i, c):
        v = wbuf.at[pl.ds(0, 15 * KH), pl.ds(0, HD)]
        rcopy(v, v, w_s.at[i], w_r.at[i, 0], twin).wait_send()
        return c

    lax.fori_loop(0, 2, kv_sent, 0)
    lax.fori_loop(2, NW, w_sent, 0)

    def a_sent(i, c):
        v = xbuf.at[pl.ds(0, 15 * FEAT), pl.ds(0, CH)]
        rcopy(v, v, a_s.at[i], a_r.at[i, 0], twin).wait_send()
        return c

    lax.fori_loop(0, NCH, a_sent, 0)
    pltpu.make_async_copy(cacheb, cache_ref, out_s.at[0]).wait()
    pltpu.make_async_copy(ctxb, ctx_ref, out_s.at[1]).wait()


def hand_on(cache_in, ctx_in, cache_ref, ctx_ref, cache_held, ctx_held, sem):
    parts = []
    for n in range(4):
        rows = pl.ds(n * ROWS // 4, ROWS // 4)
        for a, (src, held, dst) in enumerate(((cache_in, cache_held, cache_ref), (ctx_in, ctx_held, ctx_ref))):
            parts.append(
                (
                    pltpu.make_async_copy(src.at[rows, :], held.at[rows, :], sem.at[n, a, 0]),
                    pltpu.make_async_copy(held.at[rows, :], dst.at[rows, :], sem.at[n, a, 1]),
                )
            )
    for fetch, _ in parts:
        fetch.start()
    for fetch, store in parts:
        fetch.wait()
        store.start()
    for _, store in parts:
        store.wait()


def per_device(activations, norm_gain, query_gain, key_gain, query_weight, keyval_weight, lengths):
    half = np.arange(64, dtype=np.float64)
    freq = np.exp(half * (-2.0 * math.log(THETA) / HD)).astype(np.float32)
    freq = jnp.asarray(np.concatenate([freq, freq])[None, :])
    vmem = pl.BlockSpec(memory_space=pltpu.VMEM)
    hbm = pl.BlockSpec(memory_space=pl.ANY)
    dma = pltpu.SemaphoreType.DMA
    bf16, f32 = jnp.bfloat16, jnp.float32
    cache, context = pl.pallas_call(
        kernel,
        out_shape=(
            jax.ShapeDtypeStruct((ROWS, HD), bf16),
            jax.ShapeDtypeStruct((ROWS, 4 * HD), bf16),
        ),
        in_specs=[pl.BlockSpec(memory_space=pltpu.SMEM)] + [vmem] * 5 + [hbm] * 2,
        out_specs=(hbm, hbm),
        scratch_shapes=[
            pltpu.VMEM((16 * FEAT, ROWS), bf16),
            pltpu.VMEM((16 * FEAT, ROWS), bf16),
            pltpu.VMEM((8 * WROWS, 6 * HD), bf16),
            pltpu.VMEM((16 * FEAT, HD), f32),
            pltpu.VMEM((16, 16, CH), f32),
            pltpu.VMEM((16, CH), f32),
            pltpu.VMEM((ROWS, HD), jnp.int32),
            pltpu.VMEM((ROWS, HD), f32),
            pltpu.VMEM((ROWS, HD), f32),
            pltpu.VMEM((ROWS, HD), bf16),
            pltpu.VMEM((ROWS, 2 * HD), bf16),
            pltpu.VMEM((ROWS, HD), bf16),
            pltpu.VMEM((ROWS, 4 * HD), bf16),
            dma((2,)), dma, dma, dma((2,)),
            dma((NCH,)), dma((NCH, 6)), dma((NW,)), dma((NW, 6)),
        ],
        compiler_params=pltpu.CompilerParams(
            collective_id=0, has_side_effects=True, vmem_limit_bytes=56 * 2**20
        ),
        cost_estimate=pl.CostEstimate(
            flops=2 * ROWS * 5120 * 768, bytes_accessed=4 * 2**20, transcendentals=4 * ROWS * ROWS
        ),
    )(
        lengths,
        activations.T,
        norm_gain[None, :],
        freq,
        query_gain[None, :],
        key_gain[None, :],
        query_weight,
        keyval_weight,
    )
    return pl.pallas_call(
        hand_on,
        out_shape=(
            jax.ShapeDtypeStruct((ROWS, HD), bf16),
            jax.ShapeDtypeStruct((ROWS, 4 * HD), bf16),
        ),
        in_specs=[hbm] * 2,
        out_specs=(hbm, hbm),
        scratch_shapes=[
            pltpu.VMEM((ROWS, HD), bf16),
            pltpu.VMEM((ROWS, 4 * HD), bf16),
            dma((4, 2, 2)),
        ],
        compiler_params=pltpu.CompilerParams(vmem_limit_bytes=60 * 2**20),
    )(cache, context)


def solution(mesh):
    placed = (P("grp", "tp"), P(), P(), P(), P("grp", "tp"), P("grp", "tp"), P())
    return jax.shard_map(
        per_device,
        mesh=mesh,
        in_specs=placed,
        out_specs=(P("grp", "tp"), P("grp", "tp")),
        check_vma=False,
    )
```
